128 devices in a mesh: rows: 16 (over y, x), cols: 8 (over z, core).
Axes of the slice: x: 4, y: 4, z: 4, core: 2. Of those that a mesh axis runs over, the one named last changes fastest.
Arguments:
- matrix: float32 [32768, 1024], P('rows', 'cols'), may hold values from -48 to 48
- partners: int32 [2, 8], replicated, may hold values from 0 to 7, each once within a row
Outputs:
- rotated: float32 [32768, 1024], P('rows', 'cols')
The draws below stay inside these ranges and needn't reach their ends.
Inputs may be any that keep to these rules, and one draw needn't show every extreme that they name: Each row of partners names every block once.
All inputs are finite; a program needn't handle non-finite values.
Results may differ from the reference program's by a relative error of at most 0.00028.
Values sent between devices are 32-bit elements; how exact they have to be, the bound alone decides.
A program may use at most 64 MiB of HBM per device.

```python
import jax
import jax.numpy as jnp
from jax import lax

BLOCK = 128
CYCLE = 3
MATCHED = 2
STEPS = 12
M = 32768
N = 1024
N_COLS = 8


def draw_matrix(key, part):
    keys = jax.random.split(jax.random.fold_in(key, 71), 4)
    base = jnp.clip(jax.random.normal(keys[0], (M, N), jnp.float32), -5.0, 5.0)
    mixed = base + 0.5 * jnp.roll(base, -BLOCK, axis=1) + 0.4 * jnp.roll(base, -2 * BLOCK, axis=1) + 0.3 * jnp.roll(base, -3 * BLOCK, axis=1)
    common_rows = jnp.clip(jax.random.normal(keys[1], (M, 1), jnp.float32), -4.0, 4.0)
    common_cols = jnp.clip(jax.random.normal(keys[2], (1, N), jnp.float32), -4.0, 4.0)
    mixed = mixed + 0.3 * common_rows * common_cols
    colscale = jnp.exp(jax.random.uniform(keys[3], (1, N), jnp.float32, jnp.log(0.3), jnp.log(3.0)))
    return jnp.clip(mixed * colscale * 0.6, -48.0, 48.0)


def setup_inputs(seed: int = 0) -> dict:
    streams_of = jax.random.split(jax.random.key(seed), 3)
    matrix = draw_matrix(jax.random.fold_in(streams_of[2], 71), 0)
    partners = jax.vmap(lambda own: jax.random.permutation(own, N_COLS))(jax.random.split(streams_of[1], MATCHED)).reshape((MATCHED, N_COLS)).astype(jnp.int32)
    return dict(matrix=matrix, partners=partners)


epsilon = 1e-06
highest = lax.Precision.HIGHEST

def start_iterate(gram_full):
    order = gram_full.shape[0]
    scale = lax.rsqrt(jnp.diagonal(gram_full) + epsilon)
    normed = gram_full * scale[:, None] * scale[None, :]
    kernel = jnp.eye(order, dtype=jnp.float32) + jnp.triu(normed, 1) - jnp.tril(normed, -1)
    return kernel / jnp.sqrt(jnp.sum(kernel * kernel))

def polar_factor(start):

    def advance(counter, current):
        inner = jnp.dot(current.T, current, precision=highest)
        return 1.5 * current - 0.5 * jnp.dot(current, inner, precision=highest)
    return lax.fori_loop(0, STEPS, advance, start)

def reference(matrix, partners):
    blocks = matrix.reshape(M, N_COLS, BLOCK).transpose(1, 0, 2)
    for meeting in range(CYCLE + MATCHED):
        if meeting < CYCLE:
            order = (jnp.arange(N_COLS, dtype=jnp.int32) - (meeting + 1)) % N_COLS
        else:
            order = partners[meeting - CYCLE].astype(jnp.int32)

        def one_block(index, blocks=blocks, order=order):
            paired = jnp.concatenate([blocks[order[index]], blocks[index]], axis=1)
            gram_full = jnp.dot(paired.T, paired, precision=highest)
            rotation = polar_factor(start_iterate(gram_full))
            return jnp.dot(paired, rotation[:, BLOCK:], precision=highest)
        blocks = lax.map(one_block, jnp.arange(N_COLS, dtype=jnp.int32))
    return blocks.transpose(1, 0, 2).reshape(M, N)
```

```python
import functools
import jax, jax.numpy as jnp
from jax import lax
from jax.experimental import pallas as pl
from jax.experimental.pallas import tpu as pltpu
from jax.sharding import PartitionSpec as P

F32=jnp.float32; BF=jnp.bfloat16
W=128; NB=8; STEPS=12; MEET=5
EPS=1e-6

def split(x):
    h=x.astype(BF)
    return h,(x-h.astype(F32)).astype(BF)
def dot3(a,b):
    ah,al=a; bh,bl=b
    return jnp.dot(jnp.concatenate([ah,ah,al],1),jnp.concatenate([bh,bl,bh],0),preferred_element_type=F32)
def dot_nt(a,b):
    return lax.dot_general(a,b,(((1,),(1,)),((),())),preferred_element_type=F32)

def start(aa,ab,ba,bb):
    g=jnp.concatenate([jnp.concatenate([aa,ab],1),jnp.concatenate([ba,bb],1)],0)
    r=lax.broadcasted_iota(jnp.int32,g.shape,0); c=lax.broadcasted_iota(jnp.int32,g.shape,1)
    d=jnp.where(r==c,g,0.0)
    col=lax.rsqrt(jnp.sum(d,axis=1,keepdims=True)+EPS)
    row=lax.rsqrt(jnp.sum(d,axis=0,keepdims=True)+EPS)
    n=g*col*row
    k=jnp.where(r<c,n,jnp.where(r>c,-n,1.0))
    t=jnp.sum(jnp.sum(k*k,axis=1,keepdims=True),axis=0,keepdims=True)
    return k/jnp.sqrt(t)

def advance(x_ref,p):
    x=x_ref[p]
    s=split(x)
    h,l=s
    cross=dot_nt(h,l)
    inner=dot_nt(h,h)+(cross+cross.T)
    x_ref[p]=1.5*x-0.5*dot3(split(inner),s)

def partner(tab,m,j):
    return jnp.where(m<3,lax.rem(j-m-1+NB,NB),tab[jnp.maximum(m-3,0),j])

def meet_kernel(tab,gs,b_in,b_out,g,t,x,q,qt,bb, *, group=8, parts=('ns','gu','ap')):
    for j in range(NB):
        for i in range(NB):
            d=(j-i)%NB
            if d<=4:
                blk=gs[j%2,j//2,d]
            else:
                blk=gs[i%2,i//2,NB-d].T
            g[0,j,i*W:(i+1)*W,:]=blk
        bb[0,j]=b_in[j]
    def meeting(m,_):
        now=lax.rem(m,2); then=1-now
        def off(v): return pl.ds(pl.multiple_of(v*W,W),W)
        for j0 in range(0,NB,group):
            for j in range(j0,j0+group):
                qq=partner(tab,m,j)
                x[j]=start(g[now,qq,off(qq),:],g[now,j,off(qq),:],g[now,qq,j*W:(j+1)*W,:],g[now,j,j*W:(j+1)*W,:])
            if 'ns' in parts:
                def step(_,c):
                    for j in range(j0,j0+group): advance(x,j)
                    return c
                lax.fori_loop(0,STEPS,step,0)
        for j in range(NB):
            qq=partner(tab,m,j)
            w=x[j,:,W:]
            wh,wl=split(w)
            if 'ap' in parts:
                pair=jnp.concatenate([bb[now,qq],bb[now,j]],1)
                bb[then,j]=dot3(split(pair),(wh,wl))
            if 'gu' in parts:
                pair=jnp.concatenate([g[now,qq],g[now,j]],1)
                t[j]=dot3(split(pair),(wh,wl))
        if 'gu' in parts:
            for i in range(NB):
                qi=partner(tab,m,i)
                wt=x[i,:,W:].T
                ws=split(wt)
                rhs=jnp.concatenate([jnp.concatenate([t[j,off(qi),:],t[j,i*W:(i+1)*W,:]],0) for j in range(NB)],1)
                o=dot3(ws,split(rhs))
                for j in range(NB):
                    g[then,j,i*W:(i+1)*W,:]=o[:,j*W:(j+1)*W]
        return 0
    lax.fori_loop(0,MEET,meeting,0)
    b_out[...]=bb[MEET%2]

def meetings(tab,gs,b,**kw):
    V=pl.BlockSpec(memory_space=pltpu.VMEM)
    return pl.pallas_call(functools.partial(meet_kernel,**kw),
        out_shape=jax.ShapeDtypeStruct(b.shape,F32),
        in_specs=[pl.BlockSpec(memory_space=pltpu.SMEM),V,V],out_specs=V,
        scratch_shapes=[pltpu.VMEM((2,NB,NB*W,W),F32),pltpu.VMEM((NB,NB*W,W),F32),pltpu.VMEM((NB,2*W,2*W),F32),
          pltpu.VMEM((8,128),F32),pltpu.VMEM((8,128),F32),pltpu.VMEM((2,)+b.shape,F32)],
        compiler_params=pltpu.CompilerParams(vmem_limit_bytes=56*2**20))(tab,gs,b)


MESH = pl.DeviceIdType.MESH
SIDE = 4
SLAB = 512
HALF = SLAB // 2
SPAN = 5 * W
ROWS = 4 * SPAN
PARTS = ((0, 1024, (0, 1, 2)), (1024, 1024, (1, 2, 0)), (2048, 512, (2, 0, 1)))


def place():
    r, k = lax.axis_index("rows"), lax.axis_index("cols")
    return (lax.rem(r, SIDE), r // SIDE, k // 2), lax.rem(k, 2), k


def device(at, core):
    return (at[1] * SIDE + at[0], at[2] * 2 + core)


def moved(at, axis, by):
    new = list(at)
    new[axis] = lax.rem(at[axis] + by, SIDE)
    return tuple(new)


def greet(peers):
    barrier = pltpu.get_barrier_semaphore()
    for peer in peers:
        pl.semaphore_signal(barrier, inc=1, device_id=peer, device_id_type=MESH)
    pl.semaphore_wait(barrier, len(peers))


def remote(src, dst, send, recv, to):
    return pltpu.make_async_remote_copy(
        src_ref=src, dst_ref=dst, send_sem=send, recv_sem=recv, device_id=to, device_id_type=MESH
    )


def rows_at(start, size, unit):
    return pl.ds(pl.multiple_of(start, unit), size)


def gram_kernel(a, gs, b_out, b, high, low, part, land, *sems):
    (a_send, a_recv, f_send, f_recv, r_send, r_recv, g_send, g_recv, s_send, s_recv) = sems
    at, core, k = place()
    z = at[2]
    sibling = device(at, 1 - core)
    greet([device(moved(at, axis, by), core) for axis in range(3) for by in (1, 2, 3)] + [sibling])
    pending = []

    def go(copy):
        copy.start()
        pending.append(copy)
        return copy

    arrivals = []
    for by in (1, 2, 3):
        to = moved(at, 2, by)
        arrivals.append(go(remote(
            a.at[rows_at(to[2] * SLAB, SLAB, SLAB)], b.at[k], a_send.at[by - 1], a_recv.at[by - 1], device(to, core)
        )))
    own = rows_at(z * SLAB, SLAB, SLAB)
    across = [go(remote(a.at[own], b.at[k], f_send.at[0], f_recv.at[0], sibling))]

    def settle(block, value):
        h, l = split(value)
        high[block] = h
        low[block] = l

    settle(k, a[own, :])
    b_out[k] = a[rows_at(z * SLAB + core * HALF, HALF, HALF), :]

    def half_of(block):
        b_out[block] = b[block, rows_at(core * HALF, HALF, HALF), :]

    for by in (1, 2, 3):
        block = lax.rem(z + SIDE - by, SIDE) * 2 + core
        arrivals[by - 1].wait_recv()
        across.append(go(remote(b.at[block], b.at[block], f_send.at[by], f_recv.at[by], sibling)))
        settle(block, b[block])
        half_of(block)
    for by in range(4):
        block = lax.rem(z + SIDE - by, SIDE) * 2 + 1 - core
        across[by].wait_recv()
        settle(block, b[block])
        half_of(block)

    for t in range(4):
        j = 2 * t + core
        ids = [lax.rem(j - d + NB, NB) for d in range(5)]
        lh = jnp.concatenate([high[i] for i in ids], 1)
        ll = jnp.concatenate([low[i] for i in ids], 1)
        rh, rl = high[j], low[j]
        part[t * SPAN:(t + 1) * SPAN, :] = lax.dot_general(
            jnp.concatenate([lh, lh, ll], 0), jnp.concatenate([rh, rl, rh], 0),
            (((0,), (0,)), ((), ())), preferred_element_type=F32,
        )

    base = [p[0] for p in PARTS]
    size = [p[1] for p in PARTS]

    def spread(p, stage):
        axis, n = PARTS[p][2][stage], size[p] // 4
        copies = []
        for by in (1, 2, 3):
            to = moved(at, axis, by)
            copies.append(go(remote(
                part.at[rows_at(base[p] + to[axis] * n, n, 8)], land.at[p, stage, by - 1, pl.ds(0, n)],
                r_send.at[p, stage, by - 1], r_recv.at[p, stage, by - 1], device(to, core),
            )))
        base[p] = base[p] + at[axis] * n
        size[p] = n
        return copies

    waiting = [spread(p, 0) for p in range(3)]
    for stage in range(3):
        for p in range(3):
            for copy in waiting[p]:
                copy.wait_recv()
            n, mine = size[p], rows_at(base[p], size[p], 8)
            total = part[mine, :]
            for by in range(3):
                total = total + land[p, stage, by, 0:n, :]
            if stage < 2:
                part[mine, :] = total
                waiting[p] = spread(p, stage + 1)
            else:
                gs[core, mine, :] = total

    def share(p, stage):
        axis, mine = PARTS[p][2][stage], rows_at(base[p], size[p], 8)
        copies = []
        for by in (1, 2, 3):
            copies.append(go(remote(
                gs.at[core, mine], gs.at[core, mine], g_send.at[p, stage, by - 1], g_recv.at[p, stage, by - 1],
                device(moved(at, axis, by), core),
            )))
        base[p] = base[p] - at[axis] * size[p]
        size[p] = size[p] * 4
        return copies

    waiting = [share(p, 2) for p in range(3)]
    last = []
    for stage in (1, 0, -1):
        for p in range(3):
            for copy in waiting[p]:
                copy.wait_recv()
            if stage >= 0:
                waiting[p] = share(p, stage)
            else:
                whole = pl.ds(PARTS[p][0], PARTS[p][1])
                last.append(go(remote(gs.at[core, whole], gs.at[core, whole], s_send.at[p], s_recv.at[p], sibling)))
    for copy in last:
        copy.wait_recv()
    for copy in pending:
        copy.wait_send()


def gram_of(a):
    vmem = pl.BlockSpec(memory_space=pltpu.VMEM)
    dma = pltpu.SemaphoreType.DMA
    return pl.pallas_call(
        gram_kernel,
        out_shape=(
            jax.ShapeDtypeStruct((2, ROWS, W), F32),
            jax.ShapeDtypeStruct((NB, HALF, W), F32),
        ),
        in_specs=[vmem],
        out_specs=(vmem, vmem),
        scratch_shapes=[
            pltpu.VMEM((NB, SLAB, W), F32),
            pltpu.VMEM((NB, SLAB, W), BF),
            pltpu.VMEM((NB, SLAB, W), BF),
            pltpu.VMEM((ROWS, W), F32),
            pltpu.VMEM((3, 3, 3, 256, W), F32),
            dma((3,)), dma((3,)), dma((4,)), dma((4,)),
            dma((3, 3, 3)), dma((3, 3, 3)), dma((3, 3, 3)), dma((3, 3, 3)), dma((3,)), dma((3,)),
        ],
        compiler_params=pltpu.CompilerParams(
            collective_id=0, has_side_effects=True, vmem_limit_bytes=48 * 2**20
        ),
    )(a)


def return_kernel(b, out, send, recv):
    at, core, k = place()
    row = at[1] * SIDE + at[0]
    peers = [lax.rem(k + by, NB) for by in range(1, NB)]
    greet([(row, peer) for peer in peers])
    mine = rows_at(k * HALF, HALF, HALF)
    copies = []
    for n, peer in enumerate(peers):
        copies.append(remote(b.at[peer], out.at[mine], send.at[n], recv.at[n], (row, peer)))
        copies[-1].start()
    out[mine, :] = b[k]
    for copy in copies:
        copy.wait()


def returned(b):
    vmem = pl.BlockSpec(memory_space=pltpu.VMEM)
    dma = pltpu.SemaphoreType.DMA
    return pl.pallas_call(
        return_kernel,
        out_shape=jax.ShapeDtypeStruct((NB * HALF, W), F32),
        in_specs=[vmem],
        out_specs=vmem,
        scratch_shapes=[dma((NB - 1,)), dma((NB - 1,))],
        compiler_params=pltpu.CompilerParams(
            collective_id=1, has_side_effects=True, vmem_limit_bytes=32 * 2**20
        ),
    )(b)


def body(matrix, partners):
    gs, b = gram_of(matrix)
    return returned(meetings(partners, gs.reshape(2, 4, 5, W, W), b))


def solution(mesh):
    placed = (P("rows", "cols"), P())
    return jax.shard_map(
        body, mesh=mesh, in_specs=placed, out_specs=P("rows", "cols"), check_vma=False
    )
```

```python
import functools
import jax, jax.numpy as jnp
from jax import lax
from jax.experimental import pallas as pl
from jax.experimental.pallas import tpu as pltpu
from jax.sharding import PartitionSpec as P

F32=jnp.float32; BF=jnp.bfloat16
W=128; NB=8; STEPS=12; CYCLE=3; MEET=5
EPS=1e-6

def split(x):
    h=x.astype(BF)
    return h,(x-h.astype(F32)).astype(BF)
def dot3(a,b):
    ah,al=a; bh,bl=b
    return jnp.dot(jnp.concatenate([ah,ah,al],1),jnp.concatenate([bh,bl,bh],0),preferred_element_type=F32)
def dot_nt(a,b):
    return lax.dot_general(a,b,(((1,),(1,)),((),())),preferred_element_type=F32)

def start(aa,ab,ba,bb):
    g=jnp.concatenate([jnp.concatenate([aa,ab],1),jnp.concatenate([ba,bb],1)],0)
    r=lax.broadcasted_iota(jnp.int32,g.shape,0); c=lax.broadcasted_iota(jnp.int32,g.shape,1)
    d=jnp.where(r==c,g,0.0)
    col=lax.rsqrt(jnp.sum(d,axis=1,keepdims=True)+EPS)
    row=lax.rsqrt(jnp.sum(d,axis=0,keepdims=True)+EPS)
    n=g*col*row
    k=jnp.where(r<c,n,jnp.where(r>c,-n,1.0))
    t=jnp.sum(jnp.sum(k*k,axis=1,keepdims=True),axis=0,keepdims=True)
    return k/jnp.sqrt(t)

def advance(x_ref,p):
    x=x_ref[p]
    s=split(x)
    h,l=s
    cross=dot_nt(h,l)
    inner=dot_nt(h,h)+(cross+cross.T)
    x_ref[p]=1.5*x-0.5*dot3(split(inner),s)

MESH = pl.DeviceIdType.MESH
SIDE = 4
SLAB = 512
HALF = SLAB // 2
SPAN = 5 * W
ROWS = 4 * SPAN
PARTS = ((0, 1024, (0, 1, 2)), (1024, 1024, (1, 2, 0)), (2048, 512, (2, 0, 1)))


def place():
    r, k = lax.axis_index("rows"), lax.axis_index("cols")
    return (lax.rem(r, SIDE), r // SIDE, k // 2), lax.rem(k, 2), k


def device(at, core):
    return (at[1] * SIDE + at[0], at[2] * 2 + core)


def moved(at, axis, by):
    new = list(at)
    new[axis] = lax.rem(at[axis] + by, SIDE)
    return tuple(new)


def greet(peers):
    barrier = pltpu.get_barrier_semaphore()
    for peer in peers:
        pl.semaphore_signal(barrier, inc=1, device_id=peer, device_id_type=MESH)
    pl.semaphore_wait(barrier, len(peers))


def remote(src, dst, send, recv, to):
    return pltpu.make_async_remote_copy(
        src_ref=src, dst_ref=dst, send_sem=send, recv_sem=recv, device_id=to, device_id_type=MESH
    )


def rows_at(start, size, unit):
    return pl.ds(pl.multiple_of(start, unit), size)


def gram_kernel(a, gs, b_out, b, high, low, part, land, *sems):
    (a_send, a_recv, f_send, f_recv, r_send, r_recv, g_send, g_recv, s_send, s_recv) = sems
    at, core, k = place()
    z = at[2]
    sibling = device(at, 1 - core)
    greet([device(moved(at, axis, by), core) for axis in range(3) for by in (1, 2, 3)] + [sibling])
    pending = []

    def go(copy):
        copy.start()
        pending.append(copy)
        return copy

    arrivals = []
    for by in (1, 2, 3):
        to = moved(at, 2, by)
        arrivals.append(go(remote(
            a.at[rows_at(to[2] * SLAB, SLAB, SLAB)], b.at[k], a_send.at[by - 1], a_recv.at[by - 1], device(to, core)
        )))
    own = rows_at(z * SLAB, SLAB, SLAB)
    across = [go(remote(a.at[own], b.at[k], f_send.at[0], f_recv.at[0], sibling))]

    def settle(block, value):
        h, l = split(value)
        high[block] = h
        low[block] = l

    settle(k, a[own, :])
    b_out[k] = a[rows_at(z * SLAB + core * HALF, HALF, HALF), :]

    def half_of(block):
        b_out[block] = b[block, rows_at(core * HALF, HALF, HALF), :]

    for by in (1, 2, 3):
        block = lax.rem(z + SIDE - by, SIDE) * 2 + core
        arrivals[by - 1].wait_recv()
        across.append(go(remote(b.at[block], b.at[block], f_send.at[by], f_recv.at[by], sibling)))
        settle(block, b[block])
        half_of(block)
    for by in range(4):
        block = lax.rem(z + SIDE - by, SIDE) * 2 + 1 - core
        across[by].wait_recv()
        settle(block, b[block])
        half_of(block)

    for t in range(4):
        j = 2 * t + core
        ids = [lax.rem(j - d + NB, NB) for d in range(5)]
        lh = jnp.concatenate([high[i] for i in ids], 1)
        ll = jnp.concatenate([low[i] for i in ids], 1)
        rh, rl = high[j], low[j]
        part[t * SPAN:(t + 1) * SPAN, :] = lax.dot_general(
            jnp.concatenate([lh, lh, ll], 0), jnp.concatenate([rh, rl, rh], 0),
            (((0,), (0,)), ((), ())), preferred_element_type=F32,
        )

    base = [p[0] for p in PARTS]
    size = [p[1] for p in PARTS]

    def spread(p, stage):
        axis, n = PARTS[p][2][stage], size[p] // 4
        copies = []
        for by in (1, 2, 3):
            to = moved(at, axis, by)
            copies.append(go(remote(
                part.at[rows_at(base[p] + to[axis] * n, n, 8)], land.at[p, stage, by - 1, pl.ds(0, n)],
                r_send.at[p, stage, by - 1], r_recv.at[p, stage, by - 1], device(to, core),
            )))
        base[p] = base[p] + at[axis] * n
        size[p] = n
        return copies

    waiting = [spread(p, 0) for p in range(3)]
    for stage in range(3):
        for p in range(3):
            for copy in waiting[p]:
                copy.wait_recv()
            n, mine = size[p], rows_at(base[p], size[p], 8)
            total = part[mine, :]
            for by in range(3):
                total = total + land[p, stage, by, 0:n, :]
            if stage < 2:
                part[mine, :] = total
                waiting[p] = spread(p, stage + 1)
            else:
                gs[core, mine, :] = total

    def share(p, stage):
        axis, mine = PARTS[p][2][stage], rows_at(base[p], size[p], 8)
        copies = []
        for by in (1, 2, 3):
            copies.append(go(remote(
                gs.at[core, mine], gs.at[core, mine], g_send.at[p, stage, by - 1], g_recv.at[p, stage, by - 1],
                device(moved(at, axis, by), core),
            )))
        base[p] = base[p] - at[axis] * size[p]
        size[p] = size[p] * 4
        return copies

    waiting = [share(p, 2) for p in range(3)]
    last = []
    for stage in (1, 0, -1):
        for p in range(3):
            for copy in waiting[p]:
                copy.wait_recv()
            if stage >= 0:
                waiting[p] = share(p, stage)
            else:
                whole = pl.ds(PARTS[p][0], PARTS[p][1])
                last.append(go(remote(gs.at[core, whole], gs.at[core, whole], s_send.at[p], s_recv.at[p], sibling)))
    for copy in last:
        copy.wait_recv()
    for copy in pending:
        copy.wait_send()


def gram_of(a):
    vmem = pl.BlockSpec(memory_space=pltpu.VMEM)
    dma = pltpu.SemaphoreType.DMA
    return pl.pallas_call(
        gram_kernel,
        out_shape=(
            jax.ShapeDtypeStruct((2, ROWS, W), F32),
            jax.ShapeDtypeStruct((NB, HALF, W), F32),
        ),
        in_specs=[vmem],
        out_specs=(vmem, vmem),
        scratch_shapes=[
            pltpu.VMEM((NB, SLAB, W), F32),
            pltpu.VMEM((NB, SLAB, W), BF),
            pltpu.VMEM((NB, SLAB, W), BF),
            pltpu.VMEM((ROWS, W), F32),
            pltpu.VMEM((3, 3, 3, 256, W), F32),
            dma((3,)), dma((3,)), dma((4,)), dma((4,)),
            dma((3, 3, 3)), dma((3, 3, 3)), dma((3, 3, 3)), dma((3, 3, 3)), dma((3,)), dma((3,)),
        ],
        compiler_params=pltpu.CompilerParams(
            collective_id=0, has_side_effects=True, vmem_limit_bytes=48 * 2**20
        ),
    )(a)


def partner(table, meeting, j):
    if meeting < CYCLE:
        return lax.rem(j - meeting - 1 + NB, NB)
    return table[meeting - CYCLE, j]


def column(g, j):
    first = j * NB
    return jnp.concatenate([g[first + i] for i in range(NB)], 0)


def corner(g, i, j):
    return g[j * NB + i]


def meet_kernel(table, gs, b_in, out, g0, g1, g2, g3, g4, x, q, t, b0, b1, q_send, q_recv, g_send, g_recv, o_send, o_recv):
    at, core, k = place()
    row = at[1] * SIDE + at[0]
    peers = [lax.rem(k + by, NB) for by in range(1, NB)]
    greet([(row, peer) for peer in peers])
    sibling = device(at, 1 - core)
    pending = []

    def go(copy):
        copy.start()
        pending.append(copy)
        return copy

    grams = (g0, g1, g2, g3, g4)
    for j in range(NB):
        for i in range(NB):
            d = (j - i) % NB
            g0[j * NB + i] = (
                gs[j % 2, j // 2, d] if d <= 4 else gs[i % 2, i // 2, NB - d].T
            )
    b_now, b_then = b_in, b0
    for m in range(MEET):
        g = grams[m]
        for n in range(4):
            j = 2 * n + core
            qq = partner(table, m, j)
            x[n] = start(corner(g, qq, qq), corner(g, qq, j), corner(g, j, qq), corner(g, j, j))

        def step(_, carry):
            for n in range(4):
                advance(x, n)
            return carry

        lax.fori_loop(0, STEPS, step, 0)
        q[m, core] = x[:, :, W:]
        swap = go(remote(q.at[m, core], q.at[m, core], q_send.at[m], q_recv.at[m], sibling))

        def project(n, m=m, g=g):
            j = 2 * n + core
            pair = jnp.concatenate([column(g, partner(table, m, j)), column(g, j)], 1)
            t[n * NB:(n + 1) * NB] = dot3(split(pair), split(q[m, core, n])).reshape(NB, W, W)

        if m < MEET - 1:
            for n in range(4):
                project(n)
        swap.wait_recv()
        if m < MEET - 1:
            turned = [split(q[m, i % 2, i // 2].T) for i in range(NB)]
            arriving = []
            for n in range(4):
                for i in range(NB):
                    pair = jnp.concatenate([t[n * NB + partner(table, m, i)], t[n * NB + i]], 0)
                    grams[m + 1][(2 * n + core) * NB + i] = dot3(turned[i], split(pair))
                done = grams[m + 1].at[pl.ds((2 * n + core) * NB, NB)]
                arriving.append(go(remote(done, done, g_send.at[m, n], g_recv.at[m, n], sibling)))
        for j in range(NB):
            pair = jnp.concatenate([b_now[partner(table, m, j)], b_now[j]], 1)
            b_then[j] = dot3(split(pair), split(q[m, j % 2, j // 2]))
        if m < MEET - 1:
            for copy in arriving:
                copy.wait_recv()
        b_now, b_then = (b0, b1) if b_then is b0 else (b1, b0)
    mine = rows_at(k * HALF, HALF, HALF)
    returning = [
        go(remote(b_now.at[peer], out.at[mine], o_send.at[n], o_recv.at[n], (row, peer)))
        for n, peer in enumerate(peers)
    ]
    out[mine, :] = b_now[k]
    for copy in returning:
        copy.wait_recv()
    for copy in pending:
        copy.wait_send()


def meetings(table, gs, b):
    vmem = pl.BlockSpec(memory_space=pltpu.VMEM)
    dma = pltpu.SemaphoreType.DMA
    return pl.pallas_call(
        meet_kernel,
        out_shape=jax.ShapeDtypeStruct((NB * HALF, W), F32),
        in_specs=[pl.BlockSpec(memory_space=pltpu.SMEM), vmem, vmem],
        out_specs=vmem,
        scratch_shapes=[pltpu.VMEM((NB * NB, W, W), F32)] * 5 + [
            pltpu.VMEM((4, 2 * W, 2 * W), F32),
            pltpu.VMEM((MEET, 2, 4, 2 * W, W), F32),
            pltpu.VMEM((4 * NB, W, W), F32),
            pltpu.VMEM((NB, HALF, W), F32),
            pltpu.VMEM((NB, HALF, W), F32),
            dma((MEET,)), dma((MEET,)), dma((MEET - 1, 4)), dma((MEET - 1, 4)), dma((NB - 1,)), dma((NB - 1,)),
        ],
        compiler_params=pltpu.CompilerParams(
            collective_id=1, has_side_effects=True, vmem_limit_bytes=56 * 2**20
        ),
    )(table, gs, b)


def body(matrix, partners):
    gs, b = gram_of(matrix)
    return meetings(partners, gs.reshape(2, 4, 5, W, W), b)


def solution(mesh):
    placed = (P("rows", "cols"), P())
    return jax.shard_map(
        body, mesh=mesh, in_specs=placed, out_specs=P("rows", "cols"), check_vma=False
    )
```

```python
import jax
import jax.numpy as jnp
from jax import lax
from jax.experimental import pallas as pl
from jax.experimental.pallas import tpu as pltpu
from jax.sharding import PartitionSpec as P

F32, BF = jnp.float32, jnp.bfloat16
MESH = pl.DeviceIdType.MESH
CYCLE = 3
MEET = 5
STEPS = 12
EPS = 1e-6
W = 128
NB = 8
OWN = NB // 2
SIDE = 4
SLAB = 512
HALF = SLAB // 2
NEAR = 5
PART = OWN * W
ROWS = NEAR * PART
ORDERS = ((0, 1, 2), (1, 2, 0), (2, 0, 1), (0, 1, 2), (1, 2, 0))
FIRST, REST = (0, 1), (2, 3, 4)


def split(x):
    high = x.astype(BF)
    return high, (x - high.astype(F32)).astype(BF)


def dot(a, b):
    return jnp.dot(a, b, preferred_element_type=F32)


def dot_nt(a, b):
    return lax.dot_general(a, b, (((1,), (1,)), ((), ())), preferred_element_type=F32)


def dot3(a, b):
    (ah, al), (bh, bl) = a, b
    return dot(jnp.concatenate([ah, ah, al], 1), jnp.concatenate([bh, bl, bh], 0))


def start(aa, ab, ba, bb):
    g = jnp.concatenate([jnp.concatenate([aa, ab], 1), jnp.concatenate([ba, bb], 1)], 0)
    r = lax.broadcasted_iota(jnp.int32, g.shape, 0)
    c = lax.broadcasted_iota(jnp.int32, g.shape, 1)
    diagonal = jnp.where(r == c, g, 0.0)
    tall = lax.rsqrt(jnp.sum(diagonal, axis=1, keepdims=True) + EPS)
    wide = lax.rsqrt(jnp.sum(diagonal, axis=0, keepdims=True) + EPS)
    normed = g * tall * wide
    k = jnp.where(r < c, normed, jnp.where(r > c, -normed, 1.0))
    total = jnp.sum(jnp.sum(k * k, axis=1, keepdims=True), axis=0, keepdims=True)
    return k / jnp.sqrt(total)


def polar_steps(x, count):
    def step(_, carry):
        now = [x[n] for n in range(OWN)]
        halves = [split(v) for v in now]
        crossed = [dot_nt(h, l) for h, l in halves]
        plain = [dot_nt(h, h) for h, _ in halves]
        inner = [split(p + (c + c.T)) for p, c in zip(plain, crossed)]
        outer = [dot3(i, h) for i, h in zip(inner, halves)]
        for n in range(OWN):
            x[n] = 1.5 * now[n] - 0.5 * outer[n]
        return carry

    lax.fori_loop(0, count, step, 0, unroll=2)


def place():
    r, k = lax.axis_index("rows"), lax.axis_index("cols")
    return (lax.rem(r, SIDE), r // SIDE, k // 2), lax.rem(k, 2), k


def device(at, core):
    return (at[1] * SIDE + at[0], at[2] * 2 + core)


def moved(at, axis, by):
    new = list(at)
    new[axis] = lax.rem(at[axis] + by, SIDE)
    return tuple(new)


def greet(peers):
    barrier = pltpu.get_barrier_semaphore()
    for peer in peers:
        pl.semaphore_signal(barrier, inc=1, device_id=peer, device_id_type=MESH)
    pl.semaphore_wait(barrier, len(peers))


def remote(src, dst, send, recv, to):
    return pltpu.make_async_remote_copy(
        src_ref=src, dst_ref=dst, send_sem=send, recv_sem=recv, device_id=to, device_id_type=MESH
    )


def rows_at(start, size, unit):
    return pl.ds(pl.multiple_of(start, unit), size)


def partner(table, meeting, j):
    if meeting < CYCLE:
        return (j + NB - meeting - 1) % NB if isinstance(j, int) else lax.rem(j + NB - meeting - 1, NB)
    return table[meeting - CYCLE, j]


def column(g, j):
    return jnp.concatenate([g[j * NB + i] for i in range(NB)], 0)


def kernel(table, a, out, b, high, low, high_t, low_t, part, land, gs, g0, g1, g2, g3, g4, x, q, th, tl, b0, b1,
           a_send, a_recv, f_send, f_recv, r_send, r_recv, s_send, s_recv, c_send, c_recv,
           q_send, q_recv, g_send, g_recv, o_send, o_recv):
    at, core, k = place()
    row, z = at[1] * SIDE + at[0], at[2]
    sibling = device(at, 1 - core)
    peers = [lax.rem(k + by, NB) for by in range(1, NB)]
    greet([(row, peer) for peer in peers] + [device(moved(at, axis, by), core) for axis in (0, 1) for by in (1, 2, 3)])
    pending = []

    def go(copy):
        copy.start()
        pending.append(copy)
        return copy

    def arrive(copies):
        for copy in copies:
            copy.wait_recv()

    arrivals = []
    for by in (1, 2, 3):
        to = moved(at, 2, by)
        arrivals.append(go(remote(
            a.at[rows_at(to[2] * SLAB, SLAB, SLAB)], b.at[k], a_send.at[by - 1], a_recv.at[by - 1], device(to, core)
        )))
    own = rows_at(z * SLAB, SLAB, SLAB)
    across = [go(remote(a.at[own], b.at[k], f_send.at[0], f_recv.at[0], sibling))]

    def settle(block, value):
        h, l = split(value)
        high[block] = h
        low[block] = l
        high_t[block] = h.T
        low_t[block] = l.T

    settle(k, a[own, :])
    b[k] = a[own, :]
    for by in (1, 2, 3):
        block = lax.rem(z + SIDE - by, SIDE) * 2 + core
        arrivals[by - 1].wait_recv()
        across.append(go(remote(b.at[block], b.at[block], f_send.at[by], f_recv.at[by], sibling)))
        settle(block, b[block])
    for by in range(4):
        block = lax.rem(z + SIDE - by, SIDE) * 2 + 1 - core
        across[by].wait_recv()
        settle(block, b[block])

    for t in range(OWN):
        j = 2 * t + core
        ids = [lax.rem(j - d + NB, NB) for d in range(NEAR)]
        left = jnp.concatenate([jnp.concatenate([high_t[i], high_t[i], low_t[i]], 1) for i in ids], 0)
        column_sum = dot(left, jnp.concatenate([high[j], low[j], high[j]], 0))
        for d in range(NEAR):
            part[d * PART + t * W:d * PART + (t + 1) * W, :] = column_sum[d * W:(d + 1) * W]

    base = [d * PART for d in range(NEAR)]
    size = [PART] * NEAR

    def spread(p, stage):
        axis, n = ORDERS[p][stage], size[p] // SIDE
        copies = []
        for by in (1, 2, 3):
            to = moved(at, axis, by)
            copies.append(go(remote(
                part.at[rows_at(base[p] + to[axis] * n, n, 8)], land.at[p, stage, by - 1, pl.ds(0, n)],
                r_send.at[p, stage, by - 1], r_recv.at[p, stage, by - 1], device(to, core),
            )))
        base[p] = base[p] + at[axis] * n
        size[p] = n
        return copies

    waiting = [spread(p, 0) for p in range(NEAR)]
    for stage in range(3):
        for p in range(NEAR):
            arrive(waiting[p])
            n, mine = size[p], rows_at(base[p], size[p], 8)
            total = part[mine, :]
            for by in range(3):
                total = total + land[p, stage, by, 0:n, :]
            if stage < 2:
                part[mine, :] = total
                waiting[p] = spread(p, stage + 1)
            else:
                gs[core, mine, :] = total

    def share(p, stage):
        axis, mine = ORDERS[p][stage], rows_at(base[p], size[p], 8)
        copies = [
            go(remote(
                gs.at[core, mine], gs.at[core, mine], s_send.at[p, stage, by - 1], s_recv.at[p, stage, by - 1],
                device(moved(at, axis, by), core),
            ))
            for by in (1, 2, 3)
        ]
        base[p] = base[p] - at[axis] * size[p]
        size[p] = size[p] * SIDE
        return copies

    def forward(p, stage):
        arrive(waiting[p])
        if stage >= 0:
            waiting[p] = share(p, stage)
        else:
            whole = pl.ds(p * PART, PART)
            waiting[p] = [go(remote(gs.at[core, whole], gs.at[core, whole], c_send.at[p], c_recv.at[p], sibling))]

    for p in range(NEAR):
        waiting[p] = share(p, 2)
    for p in FIRST + REST:
        forward(p, 1)
    for stage in (0, -1):
        for p in FIRST:
            forward(p, stage)
    for p in FIRST:
        arrive(waiting[p])

    def summed(j, d):
        return gs[lax.rem(j, 2), rows_at(d * PART + (j // 2) * W, W, W), :]

    grams = (g0, g1, g2, g3, g4)
    mine = [2 * n + core for n in range(OWN)]
    for n, j in enumerate(mine):
        before = partner(table, 0, j)
        ab = summed(j, 1)
        x[n] = start(summed(before, 0), ab, ab.T, summed(j, 0))
    polar_steps(x, 4)
    for p in REST:
        forward(p, 0)
    polar_steps(x, 4)
    for p in REST:
        forward(p, -1)
    polar_steps(x, 4)
    for p in REST:
        arrive(waiting[p])
    for j in range(NB):
        for i in range(NB):
            d = (j - i) % NB
            c, e, f = (j, d, j // 2) if d < NEAR else (i, NB - d, i // 2)
            block = gs[c % 2, e * PART + f * W:e * PART + (f + 1) * W, :]
            g0[j * NB + i] = block if d < NEAR else block.T

    half = rows_at(core * HALF, HALF, HALF)
    returning = []
    for m in range(MEET):
        g = grams[m]
        if m:
            for n, j in enumerate(mine):
                other = partner(table, m, j)
                x[n] = start(g[other * NB + other], g[j * NB + other], g[other * NB + j], g[j * NB + j])
            polar_steps(x, STEPS)
        q[m, core] = x[:, :, W:]
        swap = go(remote(q.at[m, core], q.at[m, core], q_send.at[m], q_recv.at[m], sibling))

        def rotated(j, factor, m=m):
            other = partner(table, m, j)
            if m == 0:
                pair = [b[other, half, :], b[j, half, :]]
            else:
                held = (b0, b1)[(m - 1) % 2]
                pair = [held[other], held[j]]
            return dot3(split(jnp.concatenate(pair, 1)), split(factor))

        then = (b0, b1)[m % 2]
        if m < MEET - 1:
            for n, j in enumerate(mine):
                pair = jnp.concatenate([column(g, partner(table, m, j)), column(g, j)], 1)
                h, l = split(dot3(split(pair), split(q[m, core, n])))
                th[n * NB:(n + 1) * NB] = h.reshape(NB, W, W)
                tl[n * NB:(n + 1) * NB] = l.reshape(NB, W, W)
            swap.wait_recv()
            turned = [split(q[m, i % 2, i // 2].T) for i in range(NB)]
            arriving = []
            for two in (0, 2):
                made = []
                for i in range(NB):
                    other = partner(table, m, i)
                    right = tuple(
                        jnp.concatenate([
                            jnp.concatenate([s[n * NB + other], s[n * NB + i]], 0) for n in (two, two + 1)
                        ], 1)
                        for s in (th, tl)
                    )
                    made.append(dot3(turned[i], right))
                for e, n in enumerate((two, two + 1)):
                    for i in range(NB):
                        grams[m + 1][mine[n] * NB + i] = made[i][:, e * W:(e + 1) * W]
                    done = grams[m + 1].at[pl.ds(mine[n] * NB, NB)]
                    arriving.append(go(remote(done, done, g_send.at[m, n], g_recv.at[m, n], sibling)))
            for j in range(NB):
                then[j] = rotated(j, q[m, j % 2, j // 2])
            arrive(arriving)
        else:
            swap.wait_recv()
            home = rows_at(k * HALF, HALF, HALF)
            for n, j in enumerate(peers):
                then[j] = rotated(j, q[m, lax.rem(j, 2), j // 2])
                returning.append(go(remote(then.at[j], out.at[home], o_send.at[n], o_recv.at[n], (row, j))))
            out[home, :] = rotated(k, q[m, core, z])
    arrive(returning)
    for copy in pending:
        copy.wait_send()


def body(matrix, partners):
    vmem = pl.BlockSpec(memory_space=pltpu.VMEM)
    dma = pltpu.SemaphoreType.DMA
    square = (NB * NB, W, W)
    return pl.pallas_call(
        kernel,
        out_shape=jax.ShapeDtypeStruct(matrix.shape, F32),
        in_specs=[pl.BlockSpec(memory_space=pltpu.SMEM), vmem],
        out_specs=vmem,
        scratch_shapes=[
            pltpu.VMEM((NB, SLAB, W), F32),
            pltpu.VMEM((NB, SLAB, W), BF),
            pltpu.VMEM((NB, SLAB, W), BF),
            pltpu.VMEM((NB, W, SLAB), BF),
            pltpu.VMEM((NB, W, SLAB), BF),
            pltpu.VMEM((ROWS, W), F32),
            pltpu.VMEM((NEAR, 3, 3, PART // SIDE, W), F32),
            pltpu.VMEM((2, ROWS, W), F32),
        ] + [pltpu.VMEM(square, F32)] * MEET + [
            pltpu.VMEM((OWN, 2 * W, 2 * W), F32),
            pltpu.VMEM((MEET, 2, OWN, 2 * W, W), F32),
            pltpu.VMEM((OWN * NB, W, W), BF),
            pltpu.VMEM((OWN * NB, W, W), BF),
            pltpu.VMEM((NB, HALF, W), F32),
            pltpu.VMEM((NB, HALF, W), F32),
            dma((3,)), dma((3,)), dma((4,)), dma((4,)),
            dma((NEAR, 3, 3)), dma((NEAR, 3, 3)), dma((NEAR, 3, 3)), dma((NEAR, 3, 3)), dma((NEAR,)), dma((NEAR,)),
            dma((MEET,)), dma((MEET,)), dma((MEET - 1, OWN)), dma((MEET - 1, OWN)), dma((NB - 1,)), dma((NB - 1,)),
        ],
        compiler_params=pltpu.CompilerParams(
            collective_id=0, has_side_effects=True, vmem_limit_bytes=58 * 2**20
        ),
    )(partners, matrix)


def solution(mesh):
    placed = (P("rows", "cols"), P())
    return jax.shard_map(
        body, mesh=mesh, in_specs=placed, out_specs=P("rows", "cols"), check_vma=False
    )
```

```python
import jax
import jax.numpy as jnp
from jax import lax
from jax.experimental import pallas as pl
from jax.experimental.pallas import tpu as pltpu
from jax.sharding import PartitionSpec as P

F32, BF = jnp.float32, jnp.bfloat16
MESH = pl.DeviceIdType.MESH
CYCLE = 3
STEPS = 12
EPS = 1e-6
W = 128
NB = 8
OWN = NB // 2
SIDE = 4
SLAB = 512
NEAR = 5
PART = OWN * W
LINE = PART // SIDE
UNIT = LINE // SIDE**2
ROWS = NEAR * PART
ORDERS = ((0, 1, 2), (1, 2, 0), (2, 0, 1), (0, 1, 2), (1, 2, 0))
FIRST, REST = (0, 1), (2, 3, 4)


def split(x):
    high = x.astype(BF)
    return high, (x - high.astype(F32)).astype(BF)


def dot(a, b):
    return jnp.dot(a, b, preferred_element_type=F32)


def dot_nt(a, b):
    return lax.dot_general(a, b, (((1,), (1,)), ((), ())), preferred_element_type=F32)


def dot3(a, b):
    (ah, al), (bh, bl) = a, b
    return dot(jnp.concatenate([ah, ah, al], 1), jnp.concatenate([bh, bl, bh], 0))


def start(aa, ab, ba, bb):
    g = jnp.concatenate([jnp.concatenate([aa, ab], 1), jnp.concatenate([ba, bb], 1)], 0)
    r = lax.broadcasted_iota(jnp.int32, g.shape, 0)
    c = lax.broadcasted_iota(jnp.int32, g.shape, 1)
    diagonal = jnp.where(r == c, g, 0.0)
    tall = lax.rsqrt(jnp.sum(diagonal, axis=1, keepdims=True) + EPS)
    wide = lax.rsqrt(jnp.sum(diagonal, axis=0, keepdims=True) + EPS)
    normed = g * tall * wide
    k = jnp.where(r < c, normed, jnp.where(r > c, -normed, 1.0))
    total = jnp.sum(jnp.sum(k * k, axis=1, keepdims=True), axis=0, keepdims=True)
    return k / jnp.sqrt(total)


def polar_steps(x, count, problems=OWN):
    def step(_, carry):
        now = [x[n] for n in range(problems)]
        halves = [split(v) for v in now]
        crossed = [dot_nt(h, l) for h, l in halves]
        plain = [dot_nt(h, h) for h, _ in halves]
        inner = [split(p + (c + c.T)) for p, c in zip(plain, crossed)]
        outer = [dot3(i, h) for i, h in zip(inner, halves)]
        for n in range(problems):
            x[n] = 1.5 * now[n] - 0.5 * outer[n]
        return carry

    lax.fori_loop(0, count, step, 0, unroll=2)


def place():
    r, k = lax.axis_index("rows"), lax.axis_index("cols")
    return (lax.rem(r, SIDE), r // SIDE, k // 2), lax.rem(k, 2), k


def device(at, core):
    return (at[1] * SIDE + at[0], at[2] * 2 + core)


def moved(at, axis, by):
    new = list(at)
    new[axis] = lax.rem(at[axis] + by, SIDE)
    return tuple(new)


def greet(peers):
    barrier = pltpu.get_barrier_semaphore()
    for peer in peers:
        pl.semaphore_signal(barrier, inc=1, device_id=peer, device_id_type=MESH)
    pl.semaphore_wait(barrier, len(peers))


def remote(src, dst, send, recv, to):
    return pltpu.make_async_remote_copy(
        src_ref=src, dst_ref=dst, send_sem=send, recv_sem=recv, device_id=to, device_id_type=MESH
    )


def rows_at(start, size, unit):
    return pl.ds(pl.multiple_of(start, unit), size)


def partner(table, meeting, j):
    if meeting < CYCLE:
        return (j + NB - meeting - 1) % NB if isinstance(j, int) else lax.rem(j + NB - meeting - 1, NB)
    return table[meeting - CYCLE, j]


def column(g, j, count=NB):
    return jnp.concatenate([g[j * count + i] for i in range(count)], 0)


def beside(g, other, j, count=NB):
    return split(jnp.concatenate([column(g, other, count), column(g, j, count)], 1))


def kernel(table, a, out, wide, high, low, high_t, low_t, part, land, small, gs, g0, g1, g2, g3, x, q, ql, th, tl, w2, w3, w4,
           a_send, a_recv, f_send, f_recv, r_send, r_recv, u_send, u_recv, v_send, v_recv, s_send, s_recv, c_send, c_recv,
           q_send, q_recv, g_send, g_recv, w_send, w_recv, d_send, d_recv):
    at, core, k = place()
    z = at[2]
    sibling = device(at, 1 - core)
    near = [
        (dx, dy, dz) for dx in range(SIDE) for dy in range(SIDE) for dz in range(SIDE)
        if 0 in (dx, dy, dz) and (dx or dy or dz)
    ]
    greet([sibling] + [device(moved(moved(moved(at, 0, dx), 1, dy), 2, dz), core) for dx, dy, dz in near])
    pending = []

    def go(copy):
        copy.start()
        pending.append(copy)
        return copy

    def arrive(copies):
        for copy in copies:
            copy.wait_recv()

    def slab(where):
        return rows_at(where * SLAB, SLAB, SLAB)

    arrivals = []
    for by in (1, 2, 3):
        to = moved(at, 2, by)
        arrivals.append(go(remote(
            a.at[slab(to[2])], wide.at[k, slab(to[2])], a_send.at[by - 1], a_recv.at[by - 1], device(to, core)
        )))
    own = slab(z)
    across = [go(remote(a.at[own], wide.at[k, own], f_send.at[0], f_recv.at[0], sibling))]

    def settle(block, value):
        h, l = split(value)
        high[block] = h
        low[block] = l
        high_t[block] = h.T
        low_t[block] = l.T

    settle(k, a[own, :])
    wide[k] = a[...]
    for by in (1, 2, 3):
        block = lax.rem(z + SIDE - by, SIDE) * 2 + core
        arrivals[by - 1].wait_recv()
        across.append(go(remote(
            wide.at[block, own], wide.at[block, own], f_send.at[by], f_recv.at[by], sibling
        )))
        settle(block, wide[block, own, :])
    for by in range(4):
        block = lax.rem(z + SIDE - by, SIDE) * 2 + 1 - core
        across[by].wait_recv()
        settle(block, wide[block, own, :])

    for t in range(OWN):
        j = 2 * t + core
        ids = [lax.rem(j - d + NB, NB) for d in range(NEAR)]
        left = jnp.concatenate([jnp.concatenate([high_t[i], high_t[i], low_t[i]], 1) for i in ids], 0)
        column_sum = dot(left, jnp.concatenate([high[j], low[j], high[j]], 0))
        for d in range(NEAR):
            part[d * PART + t * W:d * PART + (t + 1) * W, :] = column_sum[d * W:(d + 1) * W]

    def line(p):
        axis = ORDERS[p][0]
        return [(by, moved(at, axis, by)) for by in (1, 2, 3)]

    def plane(p):
        _, one, two = ORDERS[p]
        return [
            (u * SIDE + v, moved(moved(at, one, u), two, v)) for u in range(SIDE) for v in range(SIDE) if u or v
        ]

    def strip(p, where):
        return p * PART + where[ORDERS[p][0]] * LINE

    def grain(p, where):
        _, one, two = ORDERS[p]
        return strip(p, at) + (where[one] * SIDE + where[two]) * UNIT

    waiting = [
        [
            go(remote(
                part.at[rows_at(strip(p, to), LINE, 8)], land.at[p, by - 1],
                r_send.at[p, by - 1], r_recv.at[p, by - 1], device(to, core),
            ))
            for by, to in line(p)
        ]
        for p in range(NEAR)
    ]
    for p in range(NEAR):
        arrive(waiting[p])
        mine = rows_at(strip(p, at), LINE, 8)
        part[mine, :] = part[mine, :] + land[p, 0] + land[p, 1] + land[p, 2]
        waiting[p] = [
            go(remote(
                part.at[rows_at(grain(p, to), UNIT, 8)], small.at[p, by - 1],
                u_send.at[p, by - 1], u_recv.at[p, by - 1], device(to, core),
            ))
            for by, to in plane(p)
        ]
    for p in range(NEAR):
        arrive(waiting[p])
        mine = rows_at(grain(p, at), UNIT, 8)
        total = part[mine, :]
        for by in range(SIDE * SIDE - 1):
            total = total + small[p, by]
        gs[core, mine, :] = total
        done = gs.at[core, mine]
        waiting[p] = [
            go(remote(done, done, v_send.at[p, by - 1], v_recv.at[p, by - 1], device(to, core)))
            for by, to in plane(p)
        ]

    def widen(p):
        arrive(waiting[p])
        done = gs.at[core, rows_at(strip(p, at), LINE, 8)]
        waiting[p] = [
            go(remote(done, done, s_send.at[p, by - 1], s_recv.at[p, by - 1], device(to, core)))
            for by, to in line(p)
        ]

    def cross(p):
        arrive(waiting[p])
        done = gs.at[core, pl.ds(p * PART, PART)]
        waiting[p] = [go(remote(done, done, c_send.at[p], c_recv.at[p], sibling))]

    for p in FIRST:
        widen(p)
    for p in FIRST:
        cross(p)
    for p in FIRST:
        arrive(waiting[p])

    def summed(j, d):
        return gs[lax.rem(j, 2), rows_at(d * PART + (j // 2) * W, W, W), :]

    grams = (g0, g1, g2)
    mine = [2 * n + core for n in range(OWN)]
    for n, j in enumerate(mine):
        before = partner(table, 0, j)
        ab = summed(j, 1)
        x[n] = start(summed(before, 0), ab, ab.T, summed(j, 0))
    polar_steps(x, 4)
    for p in REST:
        widen(p)
    polar_steps(x, 4)
    for p in REST:
        cross(p)
    polar_steps(x, 4)
    for p in REST:
        arrive(waiting[p])
    for j in range(NB):
        for i in range(NB):
            d = (j - i) % NB
            c, e, f = (j, d, j // 2) if d < NEAR else (i, NB - d, i // 2)
            block = gs[c % 2, e * PART + f * W:e * PART + (f + 1) * W, :]
            g0[j * NB + i] = block if d < NEAR else block.T

    coming = {}
    for by in (1, 2, 3):
        to = moved(at, 2, by)
        for more in (1, 2, 3):
            rest = slab(lax.rem(to[2] + more, SIDE))
            coming[by, more] = go(remote(
                a.at[rest], wide.at[k, rest], w_send.at[by - 1, more - 1], w_recv.at[by - 1, more - 1], device(to, core)
            ))

    for m in (0, 1):
        g, after = grams[m], grams[m + 1]
        if m:
            for n, j in enumerate(mine):
                other = partner(table, m, j)
                x[n] = start(g[other * NB + other], g[j * NB + other], g[other * NB + j], g[j * NB + j])
            polar_steps(x, STEPS)
        q[m, core] = x[:, :, W:]
        swap = go(remote(q.at[m, core], q.at[m, core], q_send.at[m], q_recv.at[m], sibling))
        for n, j in enumerate(mine):
            h, l = split(dot3(beside(g, partner(table, m, j), j), split(q[m, core, n])))
            th[n * NB:(n + 1) * NB] = h.reshape(NB, W, W)
            tl[n * NB:(n + 1) * NB] = l.reshape(NB, W, W)
        swap.wait_recv()
        turned = [split(q[m, i % 2, i // 2].T) for i in range(NB)]
        arriving = []
        for two in (0, 2):
            made = []
            for i in range(NB):
                other = partner(table, m, i)
                right = tuple(
                    jnp.concatenate([
                        jnp.concatenate([s[n * NB + other], s[n * NB + i]], 0) for n in (two, two + 1)
                    ], 1)
                    for s in (th, tl)
                )
                made.append(dot3(turned[i], right))
            for e, n in enumerate((two, two + 1)):
                for i in range(NB):
                    after[mine[n] * NB + i] = made[i][:, e * W:(e + 1) * W]
                done = after.at[pl.ds(mine[n] * NB, NB)]
                arriving.append(go(remote(done, done, g_send.at[m, n], g_recv.at[m, n], sibling)))
        if m:
            for j in range(NB):
                far = (j - 2) % NB
                old = [split(q[0, i % 2, i // 2]) for i in (far, j)]
                new = split(q[1, j % 2, j // 2])
                pieces = [
                    dot3(old[0], tuple(v[:W] for v in new)), dot3(old[1], tuple(v[W:] for v in new))
                ]
                for i in range(NB):
                    w2[j * NB + i] = jnp.zeros((W, W), F32)
                for e, i in enumerate(((j - 3) % NB, (j - 2) % NB, (j - 1) % NB, j)):
                    w2[j * NB + i] = pieces[e // 2][(e % 2) * W:(e % 2 + 1) * W]
        arrive(arriving)

    last = table[1, k]
    ids = [k, table[0, k], last, table[0, last]]
    others = [partner(table, 2, j) for j in ids]
    for n, (j, other) in enumerate(zip(ids, others)):
        x[n] = start(g2[other * NB + other], g2[j * NB + other], g2[other * NB + j], g2[j * NB + j])
    polar_steps(x, STEPS)
    ql[...] = x[:, :, W:]
    for n, (j, other) in enumerate(zip(ids, others)):
        factor = split(ql[n])
        h, l = split(dot3(beside(g2, other, j), factor))
        th[n * NB:(n + 1) * NB] = h.reshape(NB, W, W)
        tl[n * NB:(n + 1) * NB] = l.reshape(NB, W, W)
        w3[n * NB:(n + 1) * NB] = dot3(beside(w2, other, j), factor).reshape(NB, W, W)
    for e in range(OWN):
        right = tuple(
            jnp.concatenate([
                jnp.concatenate([s[n * NB + others[e]], s[n * NB + ids[e]]], 0) for n in range(OWN)
            ], 1)
            for s in (th, tl)
        )
        made = dot3(split(ql[e].T), right)
        for n in range(OWN):
            g3[n * OWN + e] = made[:, n * W:(n + 1) * W]

    passing = []
    for more in (1, 2, 3):
        rest = slab(lax.rem(z + more, SIDE))
        for by in range(4):
            block = lax.rem(z + SIDE - by, SIDE) * 2 + core
            if by:
                coming[by, more].wait_recv()
            passing.append(go(remote(
                wide.at[block, rest], wide.at[block, rest], d_send.at[by, more - 1], d_recv.at[by, more - 1], sibling
            )))

    pairs = ((1, 0), (3, 2))
    for n, (other, j) in enumerate(pairs):
        x[n] = start(g3[other * OWN + other], g3[j * OWN + other], g3[other * OWN + j], g3[j * OWN + j])
    polar_steps(x, STEPS, 2)
    factors = [x[n, :, W:] for n in range(2)]
    halves = [split(f) for f in factors]
    tall = [dot3(beside(g3, other, j, OWN), h) for (other, j), h in zip(pairs, halves)]
    corners = [
        [
            dot3(split(factors[e].T), split(jnp.concatenate([
                tall[n][other * W:(other + 1) * W], tall[n][j * W:(j + 1) * W]
            ], 0)))
            for n in range(2)
        ]
        for e, (other, j) in enumerate(pairs)
    ]
    for n, (other, j) in enumerate(pairs):
        w4[n * NB:(n + 1) * NB] = dot3(beside(w3, other, j), halves[n]).reshape(NB, W, W)
    x[0] = start(corners[1][1], corners[1][0], corners[0][1], corners[0][0])
    polar_steps(x, STEPS, 1)
    wh, wl = split(dot3(beside(w4, 1, 0), split(x[0, :, W:])))
    w_right = jnp.concatenate([wh, wl, wh], 0)
    arrive(passing)

    def rotate(turn, carry):
        tile = rows_at(turn * SLAB, SLAB, SLAB)
        lh, ll = split(jnp.concatenate([wide[i, tile, :] for i in range(NB)], 1))
        out[tile, :] = dot(jnp.concatenate([lh, lh, ll], 1), w_right)
        return carry

    lax.fori_loop(0, SIDE, rotate, 0)
    for copy in pending:
        copy.wait_send()


def body(matrix, partners):
    vmem = pl.BlockSpec(memory_space=pltpu.VMEM)
    dma = pltpu.SemaphoreType.DMA
    square = (NB * NB, W, W)
    quarter = (OWN * NB, W, W)
    return pl.pallas_call(
        kernel,
        out_shape=jax.ShapeDtypeStruct(matrix.shape, F32),
        in_specs=[pl.BlockSpec(memory_space=pltpu.SMEM), vmem],
        out_specs=vmem,
        scratch_shapes=[
            pltpu.VMEM((NB, SIDE * SLAB, W), F32),
            pltpu.VMEM((NB, SLAB, W), BF),
            pltpu.VMEM((NB, SLAB, W), BF),
            pltpu.VMEM((NB, W, SLAB), BF),
            pltpu.VMEM((NB, W, SLAB), BF),
            pltpu.VMEM((ROWS, W), F32),
            pltpu.VMEM((NEAR, 3, LINE, W), F32),
            pltpu.VMEM((NEAR, SIDE**2 - 1, UNIT, W), F32),
            pltpu.VMEM((2, ROWS, W), F32),
        ] + [pltpu.VMEM(square, F32)] * 3 + [
            pltpu.VMEM((OWN * OWN, W, W), F32),
            pltpu.VMEM((OWN, 2 * W, 2 * W), F32),
            pltpu.VMEM((2, 2, OWN, 2 * W, W), F32),
            pltpu.VMEM((OWN, 2 * W, W), F32),
            pltpu.VMEM(quarter, BF),
            pltpu.VMEM(quarter, BF),
            pltpu.VMEM(square, F32),
            pltpu.VMEM(quarter, F32),
            pltpu.VMEM((2 * NB, W, W), F32),
            dma((3,)), dma((3,)), dma((4,)), dma((4,)),
            dma((NEAR, 3)), dma((NEAR, 3)), dma((NEAR, 15)), dma((NEAR, 15)), dma((NEAR, 15)), dma((NEAR, 15)),
            dma((NEAR, 3)), dma((NEAR, 3)), dma((NEAR,)), dma((NEAR,)),
            dma((2,)), dma((2,)), dma((2, OWN)), dma((2, OWN)), dma((3, 3)), dma((3, 3)), dma((4, 3)), dma((4, 3)),
        ],
        compiler_params=pltpu.CompilerParams(
            collective_id=0, has_side_effects=True, vmem_limit_bytes=54 * 2**20
        ),
    )(partners, matrix)


def solution(mesh):
    placed = (P("rows", "cols"), P())
    return jax.shard_map(
        body, mesh=mesh, in_specs=placed, out_specs=P("rows", "cols"), check_vma=False
    )
```

```python
import jax
import jax.numpy as jnp
from jax import lax
from jax.experimental import pallas as pl
from jax.experimental.pallas import tpu as pltpu
from jax.sharding import PartitionSpec as P

F32, BF = jnp.float32, jnp.bfloat16
MESH = pl.DeviceIdType.MESH
CYCLE = 3
STEPS = 12
TURNS = 4
EPS = 1e-6
W = 128
NB = 8
OWN = NB // 2
SIDE = 4
SLAB = 512
NEAR = 5
PART = OWN * W
LINE = PART // SIDE
UNIT = LINE // SIDE**2
ROWS = NEAR * PART
ORDERS = ((0, 1, 2), (1, 2, 0), (2, 0, 1), (0, 1, 2), (1, 2, 0))
FIRST, REST = (0, 1), (2, 3, 4)


def split(x):
    high = x.astype(BF)
    return high, (x - high.astype(F32)).astype(BF)


def dot(a, b):
    return jnp.dot(a, b, preferred_element_type=F32)


def dot_nt(a, b):
    return lax.dot_general(a, b, (((1,), (1,)), ((), ())), preferred_element_type=F32)


def dot3(a, b):
    (ah, al), (bh, bl) = a, b
    return dot(jnp.concatenate([ah, ah, al], 1), jnp.concatenate([bh, bl, bh], 0))


def start(aa, ab, ba, bb):
    g = jnp.concatenate([jnp.concatenate([aa, ab], 1), jnp.concatenate([ba, bb], 1)], 0)
    r = lax.broadcasted_iota(jnp.int32, g.shape, 0)
    c = lax.broadcasted_iota(jnp.int32, g.shape, 1)
    diagonal = jnp.where(r == c, g, 0.0)
    tall = lax.rsqrt(jnp.sum(diagonal, axis=1, keepdims=True) + EPS)
    wide = lax.rsqrt(jnp.sum(diagonal, axis=0, keepdims=True) + EPS)
    normed = g * tall * wide
    k = jnp.where(r < c, normed, jnp.where(r > c, -normed, 1.0))
    total = jnp.sum(jnp.sum(k * k, axis=1, keepdims=True), axis=0, keepdims=True)
    return k / jnp.sqrt(total)


def polar_step(x, problems):
    now = [x[n] for n in range(problems)]
    halves = [split(v) for v in now]
    crossed = [dot_nt(h, l) for h, l in halves]
    plain = [dot_nt(h, h) for h, _ in halves]
    inner = [split(p + (c + c.T)) for p, c in zip(plain, crossed)]
    outer = [dot3(i, h) for i, h in zip(inner, halves)]
    for n in range(problems):
        x[n] = 1.5 * now[n] - 0.5 * outer[n]


def polar_steps(x, count, problems=OWN):
    def step(_, carry):
        polar_step(x, problems)
        return carry

    lax.fori_loop(0, count, step, 0, unroll=2)


def polar_beside(x, problems, work):
    def turn(t, carry):
        polar_step(x, problems)
        work(t)
        for _ in range(STEPS // TURNS - 1):
            polar_step(x, problems)
        return carry

    lax.fori_loop(0, TURNS, turn, 0)


def place():
    r, k = lax.axis_index("rows"), lax.axis_index("cols")
    return (lax.rem(r, SIDE), r // SIDE, k // 2), lax.rem(k, 2), k


def device(at, core):
    return (at[1] * SIDE + at[0], at[2] * 2 + core)


def moved(at, axis, by):
    new = list(at)
    new[axis] = lax.rem(at[axis] + by, SIDE)
    return tuple(new)


def greet(peers):
    barrier = pltpu.get_barrier_semaphore()
    for peer in peers:
        pl.semaphore_signal(barrier, inc=1, device_id=peer, device_id_type=MESH)
    pl.semaphore_wait(barrier, len(peers))


def remote(src, dst, send, recv, to):
    return pltpu.make_async_remote_copy(
        src_ref=src, dst_ref=dst, send_sem=send, recv_sem=recv, device_id=to, device_id_type=MESH
    )


def rows_at(start, size, unit):
    return pl.ds(pl.multiple_of(start, unit), size)


def partner(table, meeting, j):
    if meeting < CYCLE:
        return (j + NB - meeting - 1) % NB if isinstance(j, int) else lax.rem(j + NB - meeting - 1, NB)
    return table[meeting - CYCLE, j]


def column(g, j, count=NB):
    return jnp.concatenate([g[j * count + i] for i in range(count)], 0)


def beside(g, other, j, count=NB):
    return split(jnp.concatenate([column(g, other, count), column(g, j, count)], 1))


def kernel(table, a, out, wide, high, low, high_t, low_t, part, land, small, gs, g0, g1, g2, g3, x, q, ql, th, tl, w3, w4, paired,
           a_send, a_recv, f_send, f_recv, r_send, r_recv, u_send, u_recv, v_send, v_recv, s_send, s_recv, c_send, c_recv,
           q_send, q_recv, g_send, g_recv, w_send, w_recv, d_send, d_recv):
    at, core, k = place()
    z = at[2]
    sibling = device(at, 1 - core)
    near = [
        (dx, dy, dz) for dx in range(SIDE) for dy in range(SIDE) for dz in range(SIDE)
        if 0 in (dx, dy, dz) and (dx or dy or dz)
    ]
    greet([sibling] + [device(moved(moved(moved(at, 0, dx), 1, dy), 2, dz), core) for dx, dy, dz in near])
    pending = []

    def go(copy):
        copy.start()
        pending.append(copy)
        return copy

    def arrive(copies):
        for copy in copies:
            copy.wait_recv()

    def slab(where):
        return rows_at(where * SLAB, SLAB, SLAB)

    arrivals = []
    for by in (1, 2, 3):
        to = moved(at, 2, by)
        arrivals.append(go(remote(
            a.at[slab(to[2])], wide.at[k, slab(to[2])], a_send.at[by - 1], a_recv.at[by - 1], device(to, core)
        )))
    own = slab(z)
    across = [go(remote(a.at[own], wide.at[k, own], f_send.at[0], f_recv.at[0], sibling))]

    def settle(block, value):
        h, l = split(value)
        high[block] = h
        low[block] = l
        high_t[block] = h.T
        low_t[block] = l.T

    settle(k, a[own, :])
    wide[k] = a[...]
    for by in (1, 2, 3):
        block = lax.rem(z + SIDE - by, SIDE) * 2 + core
        arrivals[by - 1].wait_recv()
        across.append(go(remote(
            wide.at[block, own], wide.at[block, own], f_send.at[by], f_recv.at[by], sibling
        )))
        settle(block, wide[block, own, :])
    for by in range(4):
        block = lax.rem(z + SIDE - by, SIDE) * 2 + 1 - core
        across[by].wait_recv()
        settle(block, wide[block, own, :])

    for t in range(OWN):
        j = 2 * t + core
        ids = [lax.rem(j - d + NB, NB) for d in range(NEAR)]
        left = jnp.concatenate([jnp.concatenate([high_t[i], high_t[i], low_t[i]], 1) for i in ids], 0)
        column_sum = dot(left, jnp.concatenate([high[j], low[j], high[j]], 0))
        for d in range(NEAR):
            part[d * PART + t * W:d * PART + (t + 1) * W, :] = column_sum[d * W:(d + 1) * W]

    def line(p):
        axis = ORDERS[p][0]
        return [(by, moved(at, axis, by)) for by in (1, 2, 3)]

    def plane(p):
        _, one, two = ORDERS[p]
        return [
            (u * SIDE + v, moved(moved(at, one, u), two, v)) for u in range(SIDE) for v in range(SIDE) if u or v
        ]

    def strip(p, where):
        return p * PART + where[ORDERS[p][0]] * LINE

    def grain(p, where):
        _, one, two = ORDERS[p]
        return strip(p, at) + (where[one] * SIDE + where[two]) * UNIT

    waiting = [
        [
            go(remote(
                part.at[rows_at(strip(p, to), LINE, 8)], land.at[p, by - 1],
                r_send.at[p, by - 1], r_recv.at[p, by - 1], device(to, core),
            ))
            for by, to in line(p)
        ]
        for p in range(NEAR)
    ]
    for p in range(NEAR):
        arrive(waiting[p])
        mine = rows_at(strip(p, at), LINE, 8)
        part[mine, :] = part[mine, :] + land[p, 0] + land[p, 1] + land[p, 2]
        waiting[p] = [
            go(remote(
                part.at[rows_at(grain(p, to), UNIT, 8)], small.at[p, by - 1],
                u_send.at[p, by - 1], u_recv.at[p, by - 1], device(to, core),
            ))
            for by, to in plane(p)
        ]
    for p in range(NEAR):
        arrive(waiting[p])
        mine = rows_at(grain(p, at), UNIT, 8)
        total = part[mine, :]
        for by in range(SIDE * SIDE - 1):
            total = total + small[p, by]
        gs[core, mine, :] = total
        done = gs.at[core, mine]
        waiting[p] = [
            go(remote(done, done, v_send.at[p, by - 1], v_recv.at[p, by - 1], device(to, core)))
            for by, to in plane(p)
        ]

    def widen(p):
        arrive(waiting[p])
        done = gs.at[core, rows_at(strip(p, at), LINE, 8)]
        waiting[p] = [
            go(remote(done, done, s_send.at[p, by - 1], s_recv.at[p, by - 1], device(to, core)))
            for by, to in line(p)
        ]

    def cross(p):
        arrive(waiting[p])
        done = gs.at[core, pl.ds(p * PART, PART)]
        waiting[p] = [go(remote(done, done, c_send.at[p], c_recv.at[p], sibling))]

    for p in FIRST:
        widen(p)
    for p in FIRST:
        cross(p)
    arrive(waiting[0])

    def summed(j, d):
        return gs[lax.rem(j, 2), rows_at(d * PART + (j // 2) * W, W, W), :]

    grams = (g0, g1, g2)
    mine = [2 * n + core for n in range(OWN)]
    for n, j in enumerate(mine):
        before = partner(table, 0, j)
        ab = summed(j, 1)
        x[n] = start(summed(before, 0), ab, ab.T, summed(j, 0))
    polar_steps(x, 4)
    for p in REST:
        widen(p)
    polar_steps(x, 4)
    for p in REST:
        cross(p)
    polar_steps(x, 4)
    for p in (1,) + REST:
        arrive(waiting[p])
    for j in range(NB):
        for i in range(NB):
            d = (j - i) % NB
            c, e, f = (j, d, j // 2) if d < NEAR else (i, NB - d, i // 2)
            block = gs[c % 2, e * PART + f * W:e * PART + (f + 1) * W, :]
            g0[j * NB + i] = block if d < NEAR else block.T

    coming = {}
    for by in (1, 2, 3):
        to = moved(at, 2, by)
        for more in (1, 2, 3):
            rest = slab(lax.rem(to[2] + more, SIDE))
            coming[by, more] = go(remote(
                a.at[rest], wide.at[k, rest], w_send.at[by - 1, more - 1], w_recv.at[by - 1, more - 1], device(to, core)
            ))

    w2 = g0
    for m in (0, 1):
        g, after = grams[m], grams[m + 1]
        if m:
            for n, j in enumerate(mine):
                other = partner(table, m, j)
                x[n] = start(g[other * NB + other], g[j * NB + other], g[other * NB + j], g[j * NB + j])
            polar_steps(x, STEPS)
            arrive(arriving)
        q[m, core] = x[:, :, W:]
        swap = go(remote(q.at[m, core], q.at[m, core], q_send.at[m], q_recv.at[m], sibling))
        for n, j in enumerate(mine):
            h, l = split(dot3(beside(g, partner(table, m, j), j), split(q[m, core, n])))
            th[n * NB:(n + 1) * NB] = h.reshape(NB, W, W)
            tl[n * NB:(n + 1) * NB] = l.reshape(NB, W, W)
        swap.wait_recv()
        turned = [split(q[m, i % 2, i // 2].T) for i in range(NB)]
        arriving = []
        for two in (0, 2):
            made = []
            for i in range(NB):
                other = partner(table, m, i)
                right = tuple(
                    jnp.concatenate([
                        jnp.concatenate([s[n * NB + other], s[n * NB + i]], 0) for n in (two, two + 1)
                    ], 1)
                    for s in (th, tl)
                )
                made.append(dot3(turned[i], right))
            for e, n in enumerate((two, two + 1)):
                for i in range(NB):
                    after[mine[n] * NB + i] = made[i][:, e * W:(e + 1) * W]
                done = after.at[pl.ds(mine[n] * NB, NB)]
                arriving.append(go(remote(done, done, g_send.at[m, n], g_recv.at[m, n], sibling)))
        if m:
            for j in range(NB):
                far = (j - 2) % NB
                old = [split(q[0, i % 2, i // 2]) for i in (far, j)]
                new = split(q[1, j % 2, j // 2])
                pieces = [
                    dot3(old[0], tuple(v[:W] for v in new)), dot3(old[1], tuple(v[W:] for v in new))
                ]
                for i in range(NB):
                    w2[j * NB + i] = jnp.zeros((W, W), F32)
                for e, i in enumerate(((j - 3) % NB, (j - 2) % NB, (j - 1) % NB, j)):
                    w2[j * NB + i] = pieces[e // 2][(e % 2) * W:(e % 2 + 1) * W]
    arrive(arriving)

    last = table[1, k]
    ids = [k, table[0, k], last, table[0, last]]
    others = [partner(table, 2, j) for j in ids]
    for n, (j, other) in enumerate(zip(ids, others)):
        x[n] = start(g2[other * NB + other], g2[j * NB + other], g2[other * NB + j], g2[j * NB + j])
    polar_steps(x, STEPS)
    ql[...] = x[:, :, W:]
    for n, (j, other) in enumerate(zip(ids, others)):
        h, l = split(dot3(beside(g2, other, j), split(ql[n])))
        th[n * NB:(n + 1) * NB] = h.reshape(NB, W, W)
        tl[n * NB:(n + 1) * NB] = l.reshape(NB, W, W)
    for e in range(OWN):
        right = tuple(
            jnp.concatenate([
                jnp.concatenate([s[n * NB + others[e]], s[n * NB + ids[e]]], 0) for n in range(OWN)
            ], 1)
            for s in (th, tl)
        )
        made = dot3(split(ql[e].T), right)
        for n in range(OWN):
            g3[n * OWN + e] = made[:, n * W:(n + 1) * W]

    passing = []
    for more in (1, 2, 3):
        rest = slab(lax.rem(z + more, SIDE))
        for by in range(4):
            block = lax.rem(z + SIDE - by, SIDE) * 2 + core
            if by:
                coming[by, more].wait_recv()
            passing.append(go(remote(
                wide.at[block, rest], wide.at[block, rest], d_send.at[by, more - 1], d_recv.at[by, more - 1], sibling
            )))

    pairs = ((1, 0), (3, 2))
    for n, (other, j) in enumerate(pairs):
        x[n] = start(g3[other * OWN + other], g3[j * OWN + other], g3[other * OWN + j], g3[j * OWN + j])

    def follow(t):
        j = k + (t // 2) * (last - k)
        j = j + lax.rem(t, 2) * (table[0, j] - j)
        new = dot3(beside(w2, partner(table, 2, j), j), split(ql[t]))
        w3[pl.ds(t * NB, NB)] = new.reshape(NB, W, W)

    polar_beside(x, 2, follow)
    factors = [x[n, :, W:] for n in range(2)]
    halves = [split(f) for f in factors]
    tall = [dot3(beside(g3, other, j, OWN), h) for (other, j), h in zip(pairs, halves)]
    corners = [
        [
            dot3(split(factors[e].T), split(jnp.concatenate([
                tall[n][other * W:(other + 1) * W], tall[n][j * W:(j + 1) * W]
            ], 0)))
            for n in range(2)
        ]
        for e, (other, j) in enumerate(pairs)
    ]
    for n, (other, j) in enumerate(pairs):
        w4[n * NB:(n + 1) * NB] = dot3(beside(w3, other, j), halves[n]).reshape(NB, W, W)
    x[0] = start(corners[1][1], corners[1][0], corners[0][1], corners[0][0])
    wh, wl = beside(w4, 1, 0)
    w_right = jnp.concatenate([wh, wl, wh], 0)
    arrive(passing)

    def follow_rows(t):
        tile = slab(t)
        lh, ll = split(jnp.concatenate([wide[i, tile, :] for i in range(NB)], 1))
        paired[tile, :] = dot(jnp.concatenate([lh, lh, ll], 1), w_right)

    polar_beside(x, 1, follow_rows)
    factor = split(x[0, :, W:])

    def rotate(t, carry):
        tile = slab(t)
        out[tile, :] = dot3(split(paired[tile, :]), factor)
        return carry

    lax.fori_loop(0, SIDE, rotate, 0)
    for copy in pending:
        copy.wait_send()


def body(matrix, partners):
    vmem = pl.BlockSpec(memory_space=pltpu.VMEM)
    dma = pltpu.SemaphoreType.DMA
    square = (NB * NB, W, W)
    quarter = (OWN * NB, W, W)
    return pl.pallas_call(
        kernel,
        out_shape=jax.ShapeDtypeStruct(matrix.shape, F32),
        in_specs=[pl.BlockSpec(memory_space=pltpu.SMEM), vmem],
        out_specs=vmem,
        scratch_shapes=[
            pltpu.VMEM((NB, SIDE * SLAB, W), F32),
            pltpu.VMEM((NB, SLAB, W), BF),
            pltpu.VMEM((NB, SLAB, W), BF),
            pltpu.VMEM((NB, W, SLAB), BF),
            pltpu.VMEM((NB, W, SLAB), BF),
            pltpu.VMEM((ROWS, W), F32),
            pltpu.VMEM((NEAR, 3, LINE, W), F32),
            pltpu.VMEM((NEAR, SIDE**2 - 1, UNIT, W), F32),
            pltpu.VMEM((2, ROWS, W), F32),
        ] + [pltpu.VMEM(square, F32)] * 3 + [
            pltpu.VMEM((OWN * OWN, W, W), F32),
            pltpu.VMEM((OWN, 2 * W, 2 * W), F32),
            pltpu.VMEM((2, 2, OWN, 2 * W, W), F32),
            pltpu.VMEM((OWN, 2 * W, W), F32),
            pltpu.VMEM(quarter, BF),
            pltpu.VMEM(quarter, BF),
            pltpu.VMEM(quarter, F32),
            pltpu.VMEM((2 * NB, W, W), F32),
            pltpu.VMEM((SIDE * SLAB, 2 * W), F32),
            dma((3,)), dma((3,)), dma((4,)), dma((4,)),
            dma((NEAR, 3)), dma((NEAR, 3)), dma((NEAR, 15)), dma((NEAR, 15)), dma((NEAR, 15)), dma((NEAR, 15)),
            dma((NEAR, 3)), dma((NEAR, 3)), dma((NEAR,)), dma((NEAR,)),
            dma((2,)), dma((2,)), dma((2, OWN)), dma((2, OWN)), dma((3, 3)), dma((3, 3)), dma((4, 3)), dma((4, 3)),
        ],
        compiler_params=pltpu.CompilerParams(
            collective_id=0, has_side_effects=True, vmem_limit_bytes=46 * 2**20
        ),
    )(partners, matrix)


def solution(mesh):
    placed = (P("rows", "cols"), P())
    return jax.shard_map(
        body, mesh=mesh, in_specs=placed, out_specs=P("rows", "cols"), check_vma=False
    )
```

```python
import jax
import jax.numpy as jnp
from jax import lax
from jax.experimental import pallas as pl
from jax.experimental.pallas import tpu as pltpu
from jax.sharding import PartitionSpec as P

F32, BF = jnp.float32, jnp.bfloat16
MESH = pl.DeviceIdType.MESH
CYCLE = 3
STEPS = 12
TURNS = 4
EPS = 1e-6
W = 128
NB = 8
OWN = NB // 2
SIDE = 4
SLAB = 512
NEAR = 5
PART = OWN * W
LINE = PART // SIDE
UNIT = LINE // SIDE**2
ROWS = NEAR * PART
ORDERS = ((0, 1, 2), (1, 2, 0), (2, 0, 1), (0, 1, 2), (1, 2, 0))
FIRST, REST = (0, 1), (2, 3, 4)


def split(x):
    high = x.astype(BF)
    return high, (x - high.astype(F32)).astype(BF)


def dot(a, b):
    return jnp.dot(a, b, preferred_element_type=F32)


def dot_nt(a, b):
    return lax.dot_general(a, b, (((1,), (1,)), ((), ())), preferred_element_type=F32)


def dot3(a, b):
    (ah, al), (bh, bl) = a, b
    return dot(jnp.concatenate([ah, ah, al], 1), jnp.concatenate([bh, bl, bh], 0))


def start(aa, ab, ba, bb):
    g = jnp.concatenate([jnp.concatenate([aa, ab], 1), jnp.concatenate([ba, bb], 1)], 0)
    r = lax.broadcasted_iota(jnp.int32, g.shape, 0)
    c = lax.broadcasted_iota(jnp.int32, g.shape, 1)
    diagonal = jnp.where(r == c, g, 0.0)
    tall = lax.rsqrt(jnp.sum(diagonal, axis=1, keepdims=True) + EPS)
    wide = lax.rsqrt(jnp.sum(diagonal, axis=0, keepdims=True) + EPS)
    normed = g * tall * wide
    k = jnp.where(r < c, normed, jnp.where(r > c, -normed, 1.0))
    total = jnp.sum(jnp.sum(k * k, axis=1, keepdims=True), axis=0, keepdims=True)
    return k / jnp.sqrt(total)


def polar_step(x, problems):
    now = [x[n] for n in range(problems)]
    halves = [split(v) for v in now]
    crossed = [dot_nt(h, l) for h, l in halves]
    plain = [dot_nt(h, h) for h, _ in halves]
    inner = [split(p + (c + c.T)) for p, c in zip(plain, crossed)]
    outer = [dot3(i, h) for i, h in zip(inner, halves)]
    for n in range(problems):
        x[n] = 1.5 * now[n] - 0.5 * outer[n]


def polar_steps(x, count, problems=OWN):
    def step(_, carry):
        polar_step(x, problems)
        return carry

    lax.fori_loop(0, count, step, 0, unroll=2)


def polar_beside(x, problems, work):
    def turn(t, carry):
        polar_step(x, problems)
        work(t)
        for _ in range(STEPS // TURNS - 1):
            polar_step(x, problems)
        return carry

    lax.fori_loop(0, TURNS, turn, 0)


def place():
    r, k = lax.axis_index("rows"), lax.axis_index("cols")
    return (lax.rem(r, SIDE), r // SIDE, k // 2), lax.rem(k, 2), k


def device(at, core):
    return (at[1] * SIDE + at[0], at[2] * 2 + core)


def moved(at, axis, by):
    new = list(at)
    new[axis] = lax.rem(at[axis] + by, SIDE)
    return tuple(new)


def greet(peers):
    barrier = pltpu.get_barrier_semaphore()
    for peer in peers:
        pl.semaphore_signal(barrier, inc=1, device_id=peer, device_id_type=MESH)
    pl.semaphore_wait(barrier, len(peers))


def remote(src, dst, send, recv, to):
    return pltpu.make_async_remote_copy(
        src_ref=src, dst_ref=dst, send_sem=send, recv_sem=recv, device_id=to, device_id_type=MESH
    )


def rows_at(start, size, unit):
    return pl.ds(pl.multiple_of(start, unit), size)


def partner(table, meeting, j):
    if meeting < CYCLE:
        return (j + NB - meeting - 1) % NB if isinstance(j, int) else lax.rem(j + NB - meeting - 1, NB)
    return table[meeting - CYCLE, j]


def column(g, j, count=NB):
    return jnp.concatenate([g[j * count + i] for i in range(count)], 0)


def beside(g, other, j, count=NB):
    return split(jnp.concatenate([column(g, other, count), column(g, j, count)], 1))


def kernel(table, a, out, wide, high, low, high_t, low_t, part, land, small, gs, g0, g1, g2, g3, x, q, ql, th, tl, w3, w4, paired,
           a_send, a_recv, f_send, f_recv, r_send, r_recv, u_send, u_recv, v_send, v_recv, s_send, s_recv, c_send, c_recv,
           q_send, q_recv, g_send, g_recv, w_send, w_recv, d_send, d_recv):
    at, core, k = place()
    z = at[2]
    sibling = device(at, 1 - core)
    greet([sibling] + [device(moved(at, axis, by), core) for axis in range(3) for by in (1, 2, 3)])
    pending = []

    def go(copy):
        copy.start()
        pending.append(copy)
        return copy

    def arrive(copies):
        for copy in copies:
            copy.wait_recv()

    def slab(where):
        return rows_at(where * SLAB, SLAB, SLAB)

    arrivals = []
    for by in (1, 2, 3):
        to = moved(at, 2, by)
        arrivals.append(go(remote(
            a.at[slab(to[2])], wide.at[k, slab(to[2])], a_send.at[by - 1], a_recv.at[by - 1], device(to, core)
        )))
    own = slab(z)
    across = [go(remote(a.at[own], wide.at[k, own], f_send.at[0], f_recv.at[0], sibling))]

    def settle(block, value):
        h, l = split(value)
        high[block] = h
        low[block] = l
        high_t[block] = h.T
        low_t[block] = l.T

    settle(k, a[own, :])
    wide[k] = a[...]
    for by in (1, 2, 3):
        block = lax.rem(z + SIDE - by, SIDE) * 2 + core
        arrivals[by - 1].wait_recv()
        across.append(go(remote(
            wide.at[block, own], wide.at[block, own], f_send.at[by], f_recv.at[by], sibling
        )))
        settle(block, wide[block, own, :])
    for by in range(4):
        block = lax.rem(z + SIDE - by, SIDE) * 2 + 1 - core
        across[by].wait_recv()
        settle(block, wide[block, own, :])

    for t in range(OWN):
        j = 2 * t + core
        ids = [lax.rem(j - d + NB, NB) for d in range(NEAR)]
        left = jnp.concatenate([jnp.concatenate([high_t[i], high_t[i], low_t[i]], 1) for i in ids], 0)
        column_sum = dot(left, jnp.concatenate([high[j], low[j], high[j]], 0))
        for d in range(NEAR):
            part[d * PART + t * W:d * PART + (t + 1) * W, :] = column_sum[d * W:(d + 1) * W]

    def line(p):
        axis = ORDERS[p][0]
        return [(by, moved(at, axis, by)) for by in (1, 2, 3)]

    def plane(p):
        _, one, two = ORDERS[p]
        return [
            (u * SIDE + v, moved(moved(at, one, u), two, v)) for u in range(SIDE) for v in range(SIDE) if u or v
        ]

    def strip(p, where):
        return p * PART + where[ORDERS[p][0]] * LINE

    def grain(p, where):
        _, one, two = ORDERS[p]
        return strip(p, at) + (where[one] * SIDE + where[two]) * UNIT

    waiting = [
        [
            go(remote(
                part.at[rows_at(strip(p, to), LINE, 8)], land.at[p, by - 1],
                r_send.at[p, by - 1], r_recv.at[p, by - 1], device(to, core),
            ))
            for by, to in line(p)
        ]
        for p in range(NEAR)
    ]
    for p in range(NEAR):
        arrive(waiting[p])
        mine = rows_at(strip(p, at), LINE, 8)
        part[mine, :] = part[mine, :] + land[p, 0] + land[p, 1] + land[p, 2]
        waiting[p] = [
            go(remote(
                part.at[rows_at(grain(p, to), UNIT, 8)], small.at[p, by - 1],
                u_send.at[p, by - 1], u_recv.at[p, by - 1], device(to, core),
            ))
            for by, to in plane(p)
        ]
    for p in range(NEAR):
        arrive(waiting[p])
        mine = rows_at(grain(p, at), UNIT, 8)
        total = part[mine, :]
        for by in range(SIDE * SIDE - 1):
            total = total + small[p, by]
        gs[core, mine, :] = total
        done = gs.at[core, mine]
        waiting[p] = [
            go(remote(done, done, v_send.at[p, by - 1], v_recv.at[p, by - 1], device(to, core)))
            for by, to in plane(p)
        ]

    def widen(p):
        arrive(waiting[p])
        done = gs.at[core, rows_at(strip(p, at), LINE, 8)]
        waiting[p] = [
            go(remote(done, done, s_send.at[p, by - 1], s_recv.at[p, by - 1], device(to, core)))
            for by, to in line(p)
        ]

    def cross(p):
        arrive(waiting[p])
        done = gs.at[core, pl.ds(p * PART, PART)]
        waiting[p] = [go(remote(done, done, c_send.at[p], c_recv.at[p], sibling))]

    for p in FIRST:
        widen(p)
    for p in FIRST:
        cross(p)
    arrive(waiting[0])

    def summed(j, d):
        return gs[lax.rem(j, 2), rows_at(d * PART + (j // 2) * W, W, W), :]

    grams = (g0, g1, g2)
    mine = [2 * n + core for n in range(OWN)]
    for n, j in enumerate(mine):
        before = partner(table, 0, j)
        ab = summed(j, 1)
        x[n] = start(summed(before, 0), ab, ab.T, summed(j, 0))
    polar_steps(x, 4)
    for p in REST:
        widen(p)

    coming = {}
    for by in (1, 2, 3):
        to = moved(at, 2, by)
        for more in (1, 2, 3):
            rest = slab(lax.rem(to[2] + more, SIDE))
            coming[by, more] = go(remote(
                a.at[rest], wide.at[k, rest], w_send.at[by - 1, more - 1], w_recv.at[by - 1, more - 1], device(to, core)
            ))

    polar_steps(x, 4)
    for p in REST:
        cross(p)
    polar_steps(x, 4)
    for p in (1,) + REST:
        arrive(waiting[p])
    for j in range(NB):
        for i in range(NB):
            d = (j - i) % NB
            c, e, f = (j, d, j // 2) if d < NEAR else (i, NB - d, i // 2)
            block = gs[c % 2, e * PART + f * W:e * PART + (f + 1) * W, :]
            g0[j * NB + i] = block if d < NEAR else block.T

    w2 = g0
    for m in (0, 1):
        g, after = grams[m], grams[m + 1]
        if m:
            for n, j in enumerate(mine):
                other = partner(table, m, j)
                x[n] = start(g[other * NB + other], g[j * NB + other], g[other * NB + j], g[j * NB + j])
            polar_steps(x, STEPS)
            arrive(arriving)
        q[m, core] = x[:, :, W:]
        swap = go(remote(q.at[m, core], q.at[m, core], q_send.at[m], q_recv.at[m], sibling))
        for n, j in enumerate(mine):
            h, l = split(dot3(beside(g, partner(table, m, j), j), split(q[m, core, n])))
            th[n * NB:(n + 1) * NB] = h.reshape(NB, W, W)
            tl[n * NB:(n + 1) * NB] = l.reshape(NB, W, W)
        swap.wait_recv()
        turned = [split(q[m, i % 2, i // 2].T) for i in range(NB)]
        arriving = []
        for two in (0, 2):
            made = []
            for i in range(NB):
                other = partner(table, m, i)
                right = tuple(
                    jnp.concatenate([
                        jnp.concatenate([s[n * NB + other], s[n * NB + i]], 0) for n in (two, two + 1)
                    ], 1)
                    for s in (th, tl)
                )
                made.append(dot3(turned[i], right))
            for e, n in enumerate((two, two + 1)):
                for i in range(NB):
                    after[mine[n] * NB + i] = made[i][:, e * W:(e + 1) * W]
                done = after.at[pl.ds(mine[n] * NB, NB)]
                arriving.append(go(remote(done, done, g_send.at[m, n], g_recv.at[m, n], sibling)))
        if m:
            for j in range(NB):
                far = (j - 2) % NB
                old = [split(q[0, i % 2, i // 2]) for i in (far, j)]
                new = split(q[1, j % 2, j // 2])
                pieces = [
                    dot3(old[0], tuple(v[:W] for v in new)), dot3(old[1], tuple(v[W:] for v in new))
                ]
                for i in range(NB):
                    w2[j * NB + i] = jnp.zeros((W, W), F32)
                for e, i in enumerate(((j - 3) % NB, (j - 2) % NB, (j - 1) % NB, j)):
                    w2[j * NB + i] = pieces[e // 2][(e % 2) * W:(e % 2 + 1) * W]
    arrive(arriving)

    last = table[1, k]
    ids = [k, table[0, k], last, table[0, last]]
    others = [partner(table, 2, j) for j in ids]
    for n, (j, other) in enumerate(zip(ids, others)):
        x[n] = start(g2[other * NB + other], g2[j * NB + other], g2[other * NB + j], g2[j * NB + j])
    polar_steps(x, STEPS)
    ql[...] = x[:, :, W:]
    for n, (j, other) in enumerate(zip(ids, others)):
        h, l = split(dot3(beside(g2, other, j), split(ql[n])))
        th[n * NB:(n + 1) * NB] = h.reshape(NB, W, W)
        tl[n * NB:(n + 1) * NB] = l.reshape(NB, W, W)
    for e in range(OWN):
        right = tuple(
            jnp.concatenate([
                jnp.concatenate([s[n * NB + others[e]], s[n * NB + ids[e]]], 0) for n in range(OWN)
            ], 1)
            for s in (th, tl)
        )
        made = dot3(split(ql[e].T), right)
        for n in range(OWN):
            g3[n * OWN + e] = made[:, n * W:(n + 1) * W]

    passing = []
    for more in (1, 2, 3):
        rest = slab(lax.rem(z + more, SIDE))
        for by in range(4):
            block = lax.rem(z + SIDE - by, SIDE) * 2 + core
            if by:
                coming[by, more].wait_recv()
            passing.append(go(remote(
                wide.at[block, rest], wide.at[block, rest], d_send.at[by, more - 1], d_recv.at[by, more - 1], sibling
            )))

    pairs = ((1, 0), (3, 2))
    for n, (other, j) in enumerate(pairs):
        x[n] = start(g3[other * OWN + other], g3[j * OWN + other], g3[other * OWN + j], g3[j * OWN + j])

    def follow(t):
        j = k + (t // 2) * (last - k)
        j = j + lax.rem(t, 2) * (table[0, j] - j)
        new = dot3(beside(w2, partner(table, 2, j), j), split(ql[t]))
        w3[pl.ds(t * NB, NB)] = new.reshape(NB, W, W)

    polar_beside(x, 2, follow)
    factors = [x[n, :, W:] for n in range(2)]
    halves = [split(f) for f in factors]
    tall = [dot3(beside(g3, other, j, OWN), h) for (other, j), h in zip(pairs, halves)]
    corners = [
        [
            dot3(split(factors[e].T), split(jnp.concatenate([
                tall[n][other * W:(other + 1) * W], tall[n][j * W:(j + 1) * W]
            ], 0)))
            for n in range(2)
        ]
        for e, (other, j) in enumerate(pairs)
    ]
    for n, (other, j) in enumerate(pairs):
        w4[n * NB:(n + 1) * NB] = dot3(beside(w3, other, j), halves[n]).reshape(NB, W, W)
    x[0] = start(corners[1][1], corners[1][0], corners[0][1], corners[0][0])
    wh, wl = beside(w4, 1, 0)
    w_right = jnp.concatenate([wh, wl, wh], 0)
    arrive(passing)

    def follow_rows(t):
        tile = slab(t)
        lh, ll = split(jnp.concatenate([wide[i, tile, :] for i in range(NB)], 1))
        paired[tile, :] = dot(jnp.concatenate([lh, lh, ll], 1), w_right)

    polar_beside(x, 1, follow_rows)
    factor = split(x[0, :, W:])

    def rotate(t, carry):
        tile = slab(t)
        out[tile, :] = dot3(split(paired[tile, :]), factor)
        return carry

    lax.fori_loop(0, SIDE, rotate, 0)
    for copy in pending:
        copy.wait_send()


def body(matrix, partners):
    vmem = pl.BlockSpec(memory_space=pltpu.VMEM)
    dma = pltpu.SemaphoreType.DMA
    square = (NB * NB, W, W)
    quarter = (OWN * NB, W, W)
    return pl.pallas_call(
        kernel,
        out_shape=jax.ShapeDtypeStruct(matrix.shape, F32),
        in_specs=[pl.BlockSpec(memory_space=pltpu.SMEM), vmem],
        out_specs=vmem,
        scratch_shapes=[
            pltpu.VMEM((NB, SIDE * SLAB, W), F32),
            pltpu.VMEM((NB, SLAB, W), BF),
            pltpu.VMEM((NB, SLAB, W), BF),
            pltpu.VMEM((NB, W, SLAB), BF),
            pltpu.VMEM((NB, W, SLAB), BF),
            pltpu.VMEM((ROWS, W), F32),
            pltpu.VMEM((NEAR, 3, LINE, W), F32),
            pltpu.VMEM((NEAR, SIDE**2 - 1, UNIT, W), F32),
            pltpu.VMEM((2, ROWS, W), F32),
        ] + [pltpu.VMEM(square, F32)] * 3 + [
            pltpu.VMEM((OWN * OWN, W, W), F32),
            pltpu.VMEM((OWN, 2 * W, 2 * W), F32),
            pltpu.VMEM((2, 2, OWN, 2 * W, W), F32),
            pltpu.VMEM((OWN, 2 * W, W), F32),
            pltpu.VMEM(quarter, BF),
            pltpu.VMEM(quarter, BF),
            pltpu.VMEM(quarter, F32),
            pltpu.VMEM((2 * NB, W, W), F32),
            pltpu.VMEM((SIDE * SLAB, 2 * W), F32),
            dma((3,)), dma((3,)), dma((4,)), dma((4,)),
            dma((NEAR, 3)), dma((NEAR, 3)), dma((NEAR, 15)), dma((NEAR, 15)), dma((NEAR, 15)), dma((NEAR, 15)),
            dma((NEAR, 3)), dma((NEAR, 3)), dma((NEAR,)), dma((NEAR,)),
            dma((2,)), dma((2,)), dma((2, OWN)), dma((2, OWN)), dma((3, 3)), dma((3, 3)), dma((4, 3)), dma((4, 3)),
        ],
        compiler_params=pltpu.CompilerParams(
            collective_id=0, has_side_effects=True, vmem_limit_bytes=46 * 2**20
        ),
    )(partners, matrix)


def solution(mesh):
    placed = (P("rows", "cols"), P())
    return jax.shard_map(
        body, mesh=mesh, in_specs=placed, out_specs=P("rows", "cols"), check_vma=False
    )
```

```python
import jax
import jax.numpy as jnp
from jax import lax
from jax.experimental import pallas as pl
from jax.experimental.pallas import tpu as pltpu
from jax.sharding import PartitionSpec as P

F32, BF = jnp.float32, jnp.bfloat16
MESH = pl.DeviceIdType.MESH
CYCLE = 3
STEPS = 12
TURNS = 4
EPS = 1e-6
W = 128
NB = 8
OWN = NB // 2
SIDE = 4
SLAB = 512
NEAR = 5
PART = OWN * W
LINE = PART // SIDE
UNIT = LINE // SIDE**2
ROWS = NEAR * PART
ORDERS = ((0, 1, 2), (1, 2, 0), (2, 0, 1), (0, 1, 2), (1, 2, 0))
FIRST, REST = (0, 1), (2, 3, 4)


def split(x):
    high = x.astype(BF)
    return high, (x - high.astype(F32)).astype(BF)


def dot(a, b):
    return jnp.dot(a, b, preferred_element_type=F32)


def dot_nt(a, b):
    return lax.dot_general(a, b, (((1,), (1,)), ((), ())), preferred_element_type=F32)


def dot3(a, b):
    (ah, al), (bh, bl) = a, b
    return dot(jnp.concatenate([ah, ah, al], 1), jnp.concatenate([bh, bl, bh], 0))


def start(aa, ab, ba, bb):
    r = lax.broadcasted_iota(jnp.int32, aa.shape, 0)
    c = lax.broadcasted_iota(jnp.int32, aa.shape, 1)
    diagonals = [jnp.where(r == c, v, 0.0) for v in (aa, bb)]
    tall = [lax.rsqrt(jnp.sum(v, axis=1, keepdims=True) + EPS) for v in diagonals]
    wide = [lax.rsqrt(jnp.sum(v, axis=0, keepdims=True) + EPS) for v in diagonals]

    def skewed(v, e):
        normed = v * tall[e] * wide[e]
        return jnp.where(r < c, normed, jnp.where(r > c, -normed, 1.0))

    k = jnp.concatenate([
        jnp.concatenate([skewed(aa, 0), ab * tall[0] * wide[1]], 1),
        jnp.concatenate([-(ba * tall[1] * wide[0]), skewed(bb, 1)], 1),
    ], 0)
    total = jnp.sum(jnp.sum(k * k, axis=0, keepdims=True), axis=1, keepdims=True)
    return k * (1.0 / jnp.sqrt(total))


def polar_step(x, problems):
    now = [x[n] for n in range(problems)]
    halves = [split(v) for v in now]
    crossed = [dot_nt(h, l) for h, l in halves]
    plain = [dot_nt(h, h) for h, _ in halves]
    inner = [split(p + (c + c.T)) for p, c in zip(plain, crossed)]
    outer = [dot3(i, h) for i, h in zip(inner, halves)]
    for n in range(problems):
        x[n] = 1.5 * now[n] - 0.5 * outer[n]


def polar_steps(x, count, problems=OWN):
    def step(_, carry):
        polar_step(x, problems)
        return carry

    lax.fori_loop(0, count, step, 0, unroll=2)


def polar_beside(x, problems, work):
    def turn(t, carry):
        polar_step(x, problems)
        work(t)
        for _ in range(STEPS // TURNS - 1):
            polar_step(x, problems)
        return carry

    lax.fori_loop(0, TURNS, turn, 0)


def place():
    r, k = lax.axis_index("rows"), lax.axis_index("cols")
    return (lax.rem(r, SIDE), r // SIDE, k // 2), lax.rem(k, 2), k


def device(at, core):
    return (at[1] * SIDE + at[0], at[2] * 2 + core)


def moved(at, axis, by):
    new = list(at)
    new[axis] = lax.rem(at[axis] + by, SIDE)
    return tuple(new)


def greet(peers):
    barrier = pltpu.get_barrier_semaphore()
    for peer in peers:
        pl.semaphore_signal(barrier, inc=1, device_id=peer, device_id_type=MESH)
    pl.semaphore_wait(barrier, len(peers))


def remote(src, dst, send, recv, to):
    return pltpu.make_async_remote_copy(
        src_ref=src, dst_ref=dst, send_sem=send, recv_sem=recv, device_id=to, device_id_type=MESH
    )


def rows_at(start, size, unit):
    return pl.ds(pl.multiple_of(start, unit), size)


def partner(table, meeting, j):
    if meeting < CYCLE:
        return (j + NB - meeting - 1) % NB if isinstance(j, int) else lax.rem(j + NB - meeting - 1, NB)
    return table[meeting - CYCLE, j]


def column(g, j, count=NB):
    return jnp.concatenate([g[j * count + i] for i in range(count)], 0)


def beside(g, other, j, count=NB):
    return split(jnp.concatenate([column(g, other, count), column(g, j, count)], 1))


def kernel(table, a, out, wide, high, low, high_t, low_t, part, land, small, gs, g0, g1, g2, g3, x, q, ql, th, tl, w3, w4, paired,
           a_send, a_recv, f_send, f_recv, r_send, r_recv, u_send, u_recv, v_send, v_recv, s_send, s_recv, c_send, c_recv,
           q_send, q_recv, g_send, g_recv, w_send, w_recv, d_send, d_recv):
    at, core, k = place()
    z = at[2]
    sibling = device(at, 1 - core)
    greet([sibling] + [device(moved(at, axis, by), core) for axis in range(3) for by in (1, 2, 3)])
    pending = []

    def go(copy):
        copy.start()
        pending.append(copy)
        return copy

    def arrive(copies):
        for copy in copies:
            copy.wait_recv()

    def slab(where):
        return rows_at(where * SLAB, SLAB, SLAB)

    arrivals = []
    for by in (1, 2, 3):
        to = moved(at, 2, by)
        arrivals.append(go(remote(
            a.at[slab(to[2])], wide.at[k, slab(to[2])], a_send.at[by - 1], a_recv.at[by - 1], device(to, core)
        )))
    own = slab(z)
    across = [go(remote(a.at[own], wide.at[k, own], f_send.at[0], f_recv.at[0], sibling))]

    def settle(block, value):
        h, l = split(value)
        high[block] = h
        low[block] = l
        high_t[block] = h.T
        low_t[block] = l.T

    settle(k, a[own, :])
    wide[k] = a[...]
    for by in (1, 2, 3):
        block = lax.rem(z + SIDE - by, SIDE) * 2 + core
        arrivals[by - 1].wait_recv()
        across.append(go(remote(
            wide.at[block, own], wide.at[block, own], f_send.at[by], f_recv.at[by], sibling
        )))
        settle(block, wide[block, own, :])
    for by in range(4):
        block = lax.rem(z + SIDE - by, SIDE) * 2 + 1 - core
        across[by].wait_recv()
        settle(block, wide[block, own, :])

    for t in range(OWN):
        j = 2 * t + core
        ids = [lax.rem(j - d + NB, NB) for d in range(NEAR)]
        left = jnp.concatenate([jnp.concatenate([high_t[i], high_t[i], low_t[i]], 1) for i in ids], 0)
        column_sum = dot(left, jnp.concatenate([high[j], low[j], high[j]], 0))
        for d in range(NEAR):
            part[d * PART + t * W:d * PART + (t + 1) * W, :] = column_sum[d * W:(d + 1) * W]

    def line(p):
        axis = ORDERS[p][0]
        return [(by, moved(at, axis, by)) for by in (1, 2, 3)]

    def plane(p):
        _, one, two = ORDERS[p]
        return [
            (u * SIDE + v, moved(moved(at, one, u), two, v)) for u in range(SIDE) for v in range(SIDE) if u or v
        ]

    def strip(p, where):
        return p * PART + where[ORDERS[p][0]] * LINE

    def grain(p, where):
        _, one, two = ORDERS[p]
        return strip(p, at) + (where[one] * SIDE + where[two]) * UNIT

    waiting = [
        [
            go(remote(
                part.at[rows_at(strip(p, to), LINE, 8)], land.at[p, by - 1],
                r_send.at[p, by - 1], r_recv.at[p, by - 1], device(to, core),
            ))
            for by, to in line(p)
        ]
        for p in range(NEAR)
    ]
    for p in range(NEAR):
        arrive(waiting[p])
        mine = rows_at(strip(p, at), LINE, 8)
        part[mine, :] = part[mine, :] + land[p, 0] + land[p, 1] + land[p, 2]
        waiting[p] = [
            go(remote(
                part.at[rows_at(grain(p, to), UNIT, 8)], small.at[p, by - 1],
                u_send.at[p, by - 1], u_recv.at[p, by - 1], device(to, core),
            ))
            for by, to in plane(p)
        ]
    for p in range(NEAR):
        arrive(waiting[p])
        mine = rows_at(grain(p, at), UNIT, 8)
        total = part[mine, :]
        for by in range(SIDE * SIDE - 1):
            total = total + small[p, by]
        gs[core, mine, :] = total
        done = gs.at[core, mine]
        waiting[p] = [
            go(remote(done, done, v_send.at[p, by - 1], v_recv.at[p, by - 1], device(to, core)))
            for by, to in plane(p)
        ]

    def widen(p):
        arrive(waiting[p])
        done = gs.at[core, rows_at(strip(p, at), LINE, 8)]
        waiting[p] = [
            go(remote(done, done, s_send.at[p, by - 1], s_recv.at[p, by - 1], device(to, core)))
            for by, to in line(p)
        ]

    def cross(p):
        arrive(waiting[p])
        done = gs.at[core, pl.ds(p * PART, PART)]
        waiting[p] = [go(remote(done, done, c_send.at[p], c_recv.at[p], sibling))]

    for p in FIRST:
        widen(p)
    for p in FIRST:
        cross(p)
    arrive(waiting[0])

    def summed(j, d):
        return gs[lax.rem(j, 2), rows_at(d * PART + (j // 2) * W, W, W), :]

    grams = (g0, g1, g2)
    mine = [2 * n + core for n in range(OWN)]
    for n, j in enumerate(mine):
        before = partner(table, 0, j)
        ab = summed(j, 1)
        x[n] = start(summed(before, 0), ab, ab.T, summed(j, 0))
    polar_steps(x, 4)
    for p in REST:
        widen(p)
    polar_steps(x, 4)
    for p in REST:
        cross(p)
    polar_steps(x, 4)
    for p in (1,) + REST:
        arrive(waiting[p])
    for j in range(NB):
        for i in range(NB):
            d = (j - i) % NB
            c, e, f = (j, d, j // 2) if d < NEAR else (i, NB - d, i // 2)
            block = gs[c % 2, e * PART + f * W:e * PART + (f + 1) * W, :]
            g0[j * NB + i] = block if d < NEAR else block.T

    coming = {}
    for by in (1, 2, 3):
        to = moved(at, 2, by)
        for more in (1, 2, 3):
            rest = slab(lax.rem(to[2] + more, SIDE))
            coming[by, more] = go(remote(
                a.at[rest], wide.at[k, rest], w_send.at[by - 1, more - 1], w_recv.at[by - 1, more - 1], device(to, core)
            ))

    w2 = g0
    for m in (0, 1):
        g, after = grams[m], grams[m + 1]
        if m:
            for n, j in enumerate(mine):
                other = partner(table, m, j)
                x[n] = start(g[other * NB + other], g[j * NB + other], g[other * NB + j], g[j * NB + j])
            polar_steps(x, STEPS)
            arrive(arriving)
        q[m, core] = x[:, :, W:]
        swap = go(remote(q.at[m, core], q.at[m, core], q_send.at[m], q_recv.at[m], sibling))
        for n, j in enumerate(mine):
            h, l = split(dot3(beside(g, partner(table, m, j), j), split(q[m, core, n])))
            th[n * NB:(n + 1) * NB] = h.reshape(NB, W, W)
            tl[n * NB:(n + 1) * NB] = l.reshape(NB, W, W)
        swap.wait_recv()
        turned = [split(q[m, i % 2, i // 2].T) for i in range(NB)]
        arriving = []
        for two in (0, 2):
            made = []
            for i in range(NB):
                other = partner(table, m, i)
                right = tuple(
                    jnp.concatenate([
                        jnp.concatenate([s[n * NB + other], s[n * NB + i]], 0) for n in (two, two + 1)
                    ], 1)
                    for s in (th, tl)
                )
                made.append(dot3(turned[i], right))
            for e, n in enumerate((two, two + 1)):
                for i in range(NB):
                    after[mine[n] * NB + i] = made[i][:, e * W:(e + 1) * W]
                done = after.at[pl.ds(mine[n] * NB, NB)]
                arriving.append(go(remote(done, done, g_send.at[m, n], g_recv.at[m, n], sibling)))
        if m:
            for j in range(NB):
                far = (j - 2) % NB
                old = [split(q[0, i % 2, i // 2]) for i in (far, j)]
                new = split(q[1, j % 2, j // 2])
                pieces = [
                    dot3(old[0], tuple(v[:W] for v in new)), dot3(old[1], tuple(v[W:] for v in new))
                ]
                for i in range(NB):
                    w2[j * NB + i] = jnp.zeros((W, W), F32)
                for e, i in enumerate(((j - 3) % NB, (j - 2) % NB, (j - 1) % NB, j)):
                    w2[j * NB + i] = pieces[e // 2][(e % 2) * W:(e % 2 + 1) * W]
    arrive(arriving)

    last = table[1, k]
    ids = [k, table[0, k], last, table[0, last]]
    others = [partner(table, 2, j) for j in ids]
    for n, (j, other) in enumerate(zip(ids, others)):
        x[n] = start(g2[other * NB + other], g2[j * NB + other], g2[other * NB + j], g2[j * NB + j])
    polar_steps(x, STEPS)
    ql[...] = x[:, :, W:]
    for n, (j, other) in enumerate(zip(ids, others)):
        h, l = split(dot3(beside(g2, other, j), split(ql[n])))
        th[n * NB:(n + 1) * NB] = h.reshape(NB, W, W)
        tl[n * NB:(n + 1) * NB] = l.reshape(NB, W, W)
    for e in range(OWN):
        right = tuple(
            jnp.concatenate([
                jnp.concatenate([s[n * NB + others[e]], s[n * NB + ids[e]]], 0) for n in range(OWN)
            ], 1)
            for s in (th, tl)
        )
        made = dot3(split(ql[e].T), right)
        for n in range(OWN):
            g3[n * OWN + e] = made[:, n * W:(n + 1) * W]

    passing = []
    for more in (1, 2, 3):
        rest = slab(lax.rem(z + more, SIDE))
        for by in range(4):
            block = lax.rem(z + SIDE - by, SIDE) * 2 + core
            if by:
                coming[by, more].wait_recv()
            passing.append(go(remote(
                wide.at[block, rest], wide.at[block, rest], d_send.at[by, more - 1], d_recv.at[by, more - 1], sibling
            )))

    pairs = ((1, 0), (3, 2))
    for n, (other, j) in enumerate(pairs):
        x[n] = start(g3[other * OWN + other], g3[j * OWN + other], g3[other * OWN + j], g3[j * OWN + j])

    def follow(t):
        j = k + (t // 2) * (last - k)
        j = j + lax.rem(t, 2) * (table[0, j] - j)
        new = dot3(beside(w2, partner(table, 2, j), j), split(ql[t]))
        w3[pl.ds(t * NB, NB)] = new.reshape(NB, W, W)

    polar_beside(x, 2, follow)
    factors = [x[n, :, W:] for n in range(2)]
    halves = [split(f) for f in factors]
    tall = [dot3(beside(g3, other, j, OWN), h) for (other, j), h in zip(pairs, halves)]
    corners = [
        [
            dot3(split(factors[e].T), split(jnp.concatenate([
                tall[n][other * W:(other + 1) * W], tall[n][j * W:(j + 1) * W]
            ], 0)))
            for n in range(2)
        ]
        for e, (other, j) in enumerate(pairs)
    ]
    for n, (other, j) in enumerate(pairs):
        w4[n * NB:(n + 1) * NB] = dot3(beside(w3, other, j), halves[n]).reshape(NB, W, W)
    x[0] = start(corners[1][1], corners[1][0], corners[0][1], corners[0][0])
    wh, wl = beside(w4, 1, 0)
    w_right = jnp.concatenate([wh, wl, wh], 0)
    arrive(passing)

    def follow_rows(t):
        tile = slab(t)
        lh, ll = split(jnp.concatenate([wide[i, tile, :] for i in range(NB)], 1))
        paired[tile, :] = dot(jnp.concatenate([lh, lh, ll], 1), w_right)

    polar_beside(x, 1, follow_rows)
    factor = split(x[0, :, W:])

    def rotate(t, carry):
        tile = slab(t)
        out[tile, :] = dot3(split(paired[tile, :]), factor)
        return carry

    lax.fori_loop(0, SIDE, rotate, 0)
    for copy in pending:
        copy.wait_send()


def body(matrix, partners):
    vmem = pl.BlockSpec(memory_space=pltpu.VMEM)
    dma = pltpu.SemaphoreType.DMA
    square = (NB * NB, W, W)
    quarter = (OWN * NB, W, W)
    return pl.pallas_call(
        kernel,
        out_shape=jax.ShapeDtypeStruct(matrix.shape, F32),
        in_specs=[pl.BlockSpec(memory_space=pltpu.SMEM), vmem],
        out_specs=vmem,
        scratch_shapes=[
            pltpu.VMEM((NB, SIDE * SLAB, W), F32),
            pltpu.VMEM((NB, SLAB, W), BF),
            pltpu.VMEM((NB, SLAB, W), BF),
            pltpu.VMEM((NB, W, SLAB), BF),
            pltpu.VMEM((NB, W, SLAB), BF),
            pltpu.VMEM((ROWS, W), F32),
            pltpu.VMEM((NEAR, 3, LINE, W), F32),
            pltpu.VMEM((NEAR, SIDE**2 - 1, UNIT, W), F32),
            pltpu.VMEM((2, ROWS, W), F32),
        ] + [pltpu.VMEM(square, F32)] * 3 + [
            pltpu.VMEM((OWN * OWN, W, W), F32),
            pltpu.VMEM((OWN, 2 * W, 2 * W), F32),
            pltpu.VMEM((2, 2, OWN, 2 * W, W), F32),
            pltpu.VMEM((OWN, 2 * W, W), F32),
            pltpu.VMEM(quarter, BF),
            pltpu.VMEM(quarter, BF),
            pltpu.VMEM(quarter, F32),
            pltpu.VMEM((2 * NB, W, W), F32),
            pltpu.VMEM((SIDE * SLAB, 2 * W), F32),
            dma((3,)), dma((3,)), dma((4,)), dma((4,)),
            dma((NEAR, 3)), dma((NEAR, 3)), dma((NEAR, 15)), dma((NEAR, 15)), dma((NEAR, 15)), dma((NEAR, 15)),
            dma((NEAR, 3)), dma((NEAR, 3)), dma((NEAR,)), dma((NEAR,)),
            dma((2,)), dma((2,)), dma((2, OWN)), dma((2, OWN)), dma((3, 3)), dma((3, 3)), dma((4, 3)), dma((4, 3)),
        ],
        compiler_params=pltpu.CompilerParams(
            collective_id=0, has_side_effects=True, vmem_limit_bytes=46 * 2**20
        ),
    )(partners, matrix)


def solution(mesh):
    placed = (P("rows", "cols"), P())
    return jax.shard_map(
        body, mesh=mesh, in_specs=placed, out_specs=P("rows", "cols"), check_vma=False
    )
```

```python
import jax
import jax.numpy as jnp
from jax import lax
from jax.experimental import pallas as pl
from jax.experimental.pallas import tpu as pltpu
from jax.sharding import PartitionSpec as P

F32, BF = jnp.float32, jnp.bfloat16
MESH = pl.DeviceIdType.MESH
CYCLE = 3
STEPS = 12
TURNS = 4
EPS = 1e-6
W = 128
NB = 8
OWN = NB // 2
SIDE = 4
SLAB = 512
NEAR = 5
PART = OWN * W
LINE = PART // SIDE
UNIT = LINE // SIDE**2
ROWS = NEAR * PART
ORDERS = ((0, 1, 2), (1, 2, 0), (2, 0, 1), (0, 1, 2), (1, 2, 0))
FIRST, REST = (0, 1), (2, 3, 4)


def split(x):
    high = x.astype(BF)
    return high, (x - high.astype(F32)).astype(BF)


def dot(a, b):
    return jnp.dot(a, b, preferred_element_type=F32)


def dot_nt(a, b):
    return lax.dot_general(a, b, (((1,), (1,)), ((), ())), preferred_element_type=F32)


def dot3(a, b):
    (ah, al), (bh, bl) = a, b
    return dot(jnp.concatenate([ah, ah, al], 1), jnp.concatenate([bh, bl, bh], 0))


def start(aa, ab, ba, bb):
    r = lax.broadcasted_iota(jnp.int32, aa.shape, 0)
    c = lax.broadcasted_iota(jnp.int32, aa.shape, 1)
    diagonals = [jnp.where(r == c, v, 0.0) for v in (aa, bb)]
    tall = [lax.rsqrt(jnp.sum(v, axis=1, keepdims=True) + EPS) for v in diagonals]
    wide = [lax.rsqrt(jnp.sum(v, axis=0, keepdims=True) + EPS) for v in diagonals]

    def skewed(v, e):
        normed = v * tall[e] * wide[e]
        return jnp.where(r < c, normed, jnp.where(r > c, -normed, 1.0))

    k = jnp.concatenate([
        jnp.concatenate([skewed(aa, 0), ab * tall[0] * wide[1]], 1),
        jnp.concatenate([-(ba * tall[1] * wide[0]), skewed(bb, 1)], 1),
    ], 0)
    total = jnp.sum(jnp.sum(k * k, axis=0, keepdims=True), axis=1, keepdims=True)
    return k * (1.0 / jnp.sqrt(total))


def polar_step(x, problems):
    now = [x[n] for n in range(problems)]
    halves = [split(v) for v in now]
    crossed = [dot_nt(h, l) for h, l in halves]
    plain = [dot_nt(h, h) for h, _ in halves]
    inner = [split(p + (c + c.T)) for p, c in zip(plain, crossed)]
    outer = [dot3(i, h) for i, h in zip(inner, halves)]
    for n in range(problems):
        x[n] = 1.5 * now[n] - 0.5 * outer[n]


def polar_steps(x, count, problems=OWN):
    def step(_, carry):
        polar_step(x, problems)
        return carry

    lax.fori_loop(0, count, step, 0, unroll=4)


def polar_beside(x, problems, work):
    def turn(t, carry):
        polar_step(x, problems)
        work(t)
        for _ in range(STEPS // TURNS - 1):
            polar_step(x, problems)
        return carry

    lax.fori_loop(0, TURNS, turn, 0)


def place():
    r, k = lax.axis_index("rows"), lax.axis_index("cols")
    return (lax.rem(r, SIDE), r // SIDE, k // 2), lax.rem(k, 2), k


def device(at, core):
    return (at[1] * SIDE + at[0], at[2] * 2 + core)


def moved(at, axis, by):
    new = list(at)
    new[axis] = lax.rem(at[axis] + by, SIDE)
    return tuple(new)


def greet(peers):
    barrier = pltpu.get_barrier_semaphore()
    for peer in peers:
        pl.semaphore_signal(barrier, inc=1, device_id=peer, device_id_type=MESH)
    pl.semaphore_wait(barrier, len(peers))


def remote(src, dst, send, recv, to):
    return pltpu.make_async_remote_copy(
        src_ref=src, dst_ref=dst, send_sem=send, recv_sem=recv, device_id=to, device_id_type=MESH
    )


def rows_at(start, size, unit):
    return pl.ds(pl.multiple_of(start, unit), size)


def partner(table, meeting, j):
    if meeting < CYCLE:
        return (j + NB - meeting - 1) % NB if isinstance(j, int) else lax.rem(j + NB - meeting - 1, NB)
    return table[meeting - CYCLE, j]


def column(g, j, count=NB):
    return jnp.concatenate([g[j * count + i] for i in range(count)], 0)


def beside(g, other, j, count=NB):
    return split(jnp.concatenate([column(g, other, count), column(g, j, count)], 1))


def kernel(table, a, out, wide, high, low, high_t, low_t, part, land, small, gs, g0, g1, g2, g3, x, q, ql, th, tl, w3, w4, paired,
           a_send, a_recv, f_send, f_recv, r_send, r_recv, u_send, u_recv, v_send, v_recv, s_send, s_recv, c_send, c_recv,
           q_send, q_recv, g_send, g_recv, w_send, w_recv, d_send, d_recv):
    at, core, k = place()
    z = at[2]
    sibling = device(at, 1 - core)
    greet([sibling] + [device(moved(at, axis, by), core) for axis in range(3) for by in (1, 2, 3)])
    pending = []

    def go(copy):
        copy.start()
        pending.append(copy)
        return copy

    def arrive(copies):
        for copy in copies:
            copy.wait_recv()

    def slab(where):
        return rows_at(where * SLAB, SLAB, SLAB)

    arrivals = []
    for by in (1, 2, 3):
        to = moved(at, 2, by)
        arrivals.append(go(remote(
            a.at[slab(to[2])], wide.at[k, slab(to[2])], a_send.at[by - 1], a_recv.at[by - 1], device(to, core)
        )))
    own = slab(z)
    across = [go(remote(a.at[own], wide.at[k, own], f_send.at[0], f_recv.at[0], sibling))]

    def settle(block, value):
        h, l = split(value)
        high[block] = h
        low[block] = l
        high_t[block] = h.T
        low_t[block] = l.T

    settle(k, a[own, :])
    wide[k] = a[...]
    for by in (1, 2, 3):
        block = lax.rem(z + SIDE - by, SIDE) * 2 + core
        arrivals[by - 1].wait_recv()
        across.append(go(remote(
            wide.at[block, own], wide.at[block, own], f_send.at[by], f_recv.at[by], sibling
        )))
        settle(block, wide[block, own, :])
    for by in range(4):
        block = lax.rem(z + SIDE - by, SIDE) * 2 + 1 - core
        across[by].wait_recv()
        settle(block, wide[block, own, :])

    for t in range(OWN):
        j = 2 * t + core
        ids = [lax.rem(j - d + NB, NB) for d in range(NEAR)]
        left = jnp.concatenate([jnp.concatenate([high_t[i], high_t[i], low_t[i]], 1) for i in ids], 0)
        column_sum = dot(left, jnp.concatenate([high[j], low[j], high[j]], 0))
        for d in range(NEAR):
            part[d * PART + t * W:d * PART + (t + 1) * W, :] = column_sum[d * W:(d + 1) * W]

    def line(p):
        axis = ORDERS[p][0]
        return [(by, moved(at, axis, by)) for by in (1, 2, 3)]

    def plane(p):
        _, one, two = ORDERS[p]
        return [
            (u * SIDE + v, moved(moved(at, one, u), two, v)) for u in range(SIDE) for v in range(SIDE) if u or v
        ]

    def strip(p, where):
        return p * PART + where[ORDERS[p][0]] * LINE

    def grain(p, where):
        _, one, two = ORDERS[p]
        return strip(p, at) + (where[one] * SIDE + where[two]) * UNIT

    waiting = [
        [
            go(remote(
                part.at[rows_at(strip(p, to), LINE, 8)], land.at[p, by - 1],
                r_send.at[p, by - 1], r_recv.at[p, by - 1], device(to, core),
            ))
            for by, to in line(p)
        ]
        for p in range(NEAR)
    ]
    for p in range(NEAR):
        arrive(waiting[p])
        mine = rows_at(strip(p, at), LINE, 8)
        part[mine, :] = part[mine, :] + land[p, 0] + land[p, 1] + land[p, 2]
        waiting[p] = [
            go(remote(
                part.at[rows_at(grain(p, to), UNIT, 8)], small.at[p, by - 1],
                u_send.at[p, by - 1], u_recv.at[p, by - 1], device(to, core),
            ))
            for by, to in plane(p)
        ]
    for p in range(NEAR):
        arrive(waiting[p])
        mine = rows_at(grain(p, at), UNIT, 8)
        total = part[mine, :]
        for by in range(SIDE * SIDE - 1):
            total = total + small[p, by]
        gs[core, mine, :] = total
        done = gs.at[core, mine]
        waiting[p] = [
            go(remote(done, done, v_send.at[p, by - 1], v_recv.at[p, by - 1], device(to, core)))
            for by, to in plane(p)
        ]

    def widen(p):
        arrive(waiting[p])
        done = gs.at[core, rows_at(strip(p, at), LINE, 8)]
        waiting[p] = [
            go(remote(done, done, s_send.at[p, by - 1], s_recv.at[p, by - 1], device(to, core)))
            for by, to in line(p)
        ]

    def cross(p):
        arrive(waiting[p])
        done = gs.at[core, pl.ds(p * PART, PART)]
        waiting[p] = [go(remote(done, done, c_send.at[p], c_recv.at[p], sibling))]

    for p in FIRST:
        widen(p)
    for p in FIRST:
        cross(p)
    arrive(waiting[0])

    def summed(j, d):
        return gs[lax.rem(j, 2), rows_at(d * PART + (j // 2) * W, W, W), :]

    grams = (g0, g1, g2)
    mine = [2 * n + core for n in range(OWN)]
    for n, j in enumerate(mine):
        before = partner(table, 0, j)
        ab = summed(j, 1)
        x[n] = start(summed(before, 0), ab, ab.T, summed(j, 0))
    def lay_out(wanted):
        for j in range(NB):
            for i in range(NB):
                d = (j - i) % NB
                if d in wanted:
                    c, e, f = (j, d, j // 2) if d < NEAR else (i, NB - d, i // 2)
                    block = gs[c % 2, e * PART + f * W:e * PART + (f + 1) * W, :]
                    g0[j * NB + i] = block if d < NEAR else block.T

    polar_steps(x, 4)
    for p in REST:
        widen(p)
    arrive(waiting[1])
    polar_step(x, OWN)
    lay_out((0, 1, NB - 1))
    for _ in range(3):
        polar_step(x, OWN)
    for p in REST:
        cross(p)
    polar_steps(x, 4)
    for p in REST:
        arrive(waiting[p])
    lay_out(range(2, NB - 1))

    coming = {}
    for by in (1, 2, 3):
        to = moved(at, 2, by)
        for more in (1, 2, 3):
            rest = slab(lax.rem(to[2] + more, SIDE))
            coming[by, more] = go(remote(
                a.at[rest], wide.at[k, rest], w_send.at[by - 1, more - 1], w_recv.at[by - 1, more - 1], device(to, core)
            ))

    w2 = g0
    for m in (0, 1):
        g, after = grams[m], grams[m + 1]
        if m:
            for n, j in enumerate(mine):
                other = partner(table, m, j)
                x[n] = start(g[other * NB + other], g[j * NB + other], g[other * NB + j], g[j * NB + j])
            polar_steps(x, STEPS)
            arrive(arriving)
        q[m, core] = x[:, :, W:]
        swap = go(remote(q.at[m, core], q.at[m, core], q_send.at[m], q_recv.at[m], sibling))
        for n, j in enumerate(mine):
            h, l = split(dot3(beside(g, partner(table, m, j), j), split(q[m, core, n])))
            th[n * NB:(n + 1) * NB] = h.reshape(NB, W, W)
            tl[n * NB:(n + 1) * NB] = l.reshape(NB, W, W)
        swap.wait_recv()
        turned = [split(q[m, i % 2, i // 2].T) for i in range(NB)]
        arriving = []
        for two in (0, 2):
            made = []
            for i in range(NB):
                other = partner(table, m, i)
                right = tuple(
                    jnp.concatenate([
                        jnp.concatenate([s[n * NB + other], s[n * NB + i]], 0) for n in (two, two + 1)
                    ], 1)
                    for s in (th, tl)
                )
                made.append(dot3(turned[i], right))
            for e, n in enumerate((two, two + 1)):
                for i in range(NB):
                    after[mine[n] * NB + i] = made[i][:, e * W:(e + 1) * W]
                done = after.at[pl.ds(mine[n] * NB, NB)]
                arriving.append(go(remote(done, done, g_send.at[m, n], g_recv.at[m, n], sibling)))
        if m:
            for j in range(NB):
                far = (j - 2) % NB
                old = [split(q[0, i % 2, i // 2]) for i in (far, j)]
                new = split(q[1, j % 2, j // 2])
                pieces = [
                    dot3(old[0], tuple(v[:W] for v in new)), dot3(old[1], tuple(v[W:] for v in new))
                ]
                for i in range(NB):
                    w2[j * NB + i] = jnp.zeros((W, W), F32)
                for e, i in enumerate(((j - 3) % NB, (j - 2) % NB, (j - 1) % NB, j)):
                    w2[j * NB + i] = pieces[e // 2][(e % 2) * W:(e % 2 + 1) * W]
    arrive(arriving)

    last = table[1, k]
    ids = [k, table[0, k], last, table[0, last]]
    others = [partner(table, 2, j) for j in ids]
    for n, (j, other) in enumerate(zip(ids, others)):
        x[n] = start(g2[other * NB + other], g2[j * NB + other], g2[other * NB + j], g2[j * NB + j])
    polar_steps(x, STEPS)
    ql[...] = x[:, :, W:]
    for n, (j, other) in enumerate(zip(ids, others)):
        h, l = split(dot3(beside(g2, other, j), split(ql[n])))
        th[n * NB:(n + 1) * NB] = h.reshape(NB, W, W)
        tl[n * NB:(n + 1) * NB] = l.reshape(NB, W, W)
    for e in range(OWN):
        right = tuple(
            jnp.concatenate([
                jnp.concatenate([s[n * NB + others[e]], s[n * NB + ids[e]]], 0) for n in range(OWN)
            ], 1)
            for s in (th, tl)
        )
        made = dot3(split(ql[e].T), right)
        for n in range(OWN):
            g3[n * OWN + e] = made[:, n * W:(n + 1) * W]

    passing = []
    for more in (1, 2, 3):
        rest = slab(lax.rem(z + more, SIDE))
        for by in range(4):
            block = lax.rem(z + SIDE - by, SIDE) * 2 + core
            if by:
                coming[by, more].wait_recv()
            passing.append(go(remote(
                wide.at[block, rest], wide.at[block, rest], d_send.at[by, more - 1], d_recv.at[by, more - 1], sibling
            )))

    pairs = ((1, 0), (3, 2))
    for n, (other, j) in enumerate(pairs):
        x[n] = start(g3[other * OWN + other], g3[j * OWN + other], g3[other * OWN + j], g3[j * OWN + j])

    def follow(t):
        j = k + (t // 2) * (last - k)
        j = j + lax.rem(t, 2) * (table[0, j] - j)
        new = dot3(beside(w2, partner(table, 2, j), j), split(ql[t]))
        w3[pl.ds(t * NB, NB)] = new.reshape(NB, W, W)

    polar_beside(x, 2, follow)
    factors = [x[n, :, W:] for n in range(2)]
    halves = [split(f) for f in factors]
    tall = [dot3(beside(g3, other, j, OWN), h) for (other, j), h in zip(pairs, halves)]
    corners = [
        [
            dot3(split(factors[e].T), split(jnp.concatenate([
                tall[n][other * W:(other + 1) * W], tall[n][j * W:(j + 1) * W]
            ], 0)))
            for n in range(2)
        ]
        for e, (other, j) in enumerate(pairs)
    ]
    for n, (other, j) in enumerate(pairs):
        w4[n * NB:(n + 1) * NB] = dot3(beside(w3, other, j), halves[n]).reshape(NB, W, W)
    x[0] = start(corners[1][1], corners[1][0], corners[0][1], corners[0][0])
    wh, wl = beside(w4, 1, 0)
    w_right = jnp.concatenate([wh, wl, wh], 0)
    arrive(passing)

    def follow_rows(t):
        tile = slab(t)
        lh, ll = split(jnp.concatenate([wide[i, tile, :] for i in range(NB)], 1))
        paired[tile, :] = dot(jnp.concatenate([lh, lh, ll], 1), w_right)

    polar_beside(x, 1, follow_rows)
    factor = split(x[0, :, W:])

    def rotate(t, carry):
        tile = slab(t)
        out[tile, :] = dot3(split(paired[tile, :]), factor)
        return carry

    lax.fori_loop(0, SIDE, rotate, 0)
    for copy in pending:
        copy.wait_send()


def body(matrix, partners):
    vmem = pl.BlockSpec(memory_space=pltpu.VMEM)
    dma = pltpu.SemaphoreType.DMA
    square = (NB * NB, W, W)
    quarter = (OWN * NB, W, W)
    return pl.pallas_call(
        kernel,
        out_shape=jax.ShapeDtypeStruct(matrix.shape, F32),
        in_specs=[pl.BlockSpec(memory_space=pltpu.SMEM), vmem],
        out_specs=vmem,
        scratch_shapes=[
            pltpu.VMEM((NB, SIDE * SLAB, W), F32),
            pltpu.VMEM((NB, SLAB, W), BF),
            pltpu.VMEM((NB, SLAB, W), BF),
            pltpu.VMEM((NB, W, SLAB), BF),
            pltpu.VMEM((NB, W, SLAB), BF),
            pltpu.VMEM((ROWS, W), F32),
            pltpu.VMEM((NEAR, 3, LINE, W), F32),
            pltpu.VMEM((NEAR, SIDE**2 - 1, UNIT, W), F32),
            pltpu.VMEM((2, ROWS, W), F32),
        ] + [pltpu.VMEM(square, F32)] * 3 + [
            pltpu.VMEM((OWN * OWN, W, W), F32),
            pltpu.VMEM((OWN, 2 * W, 2 * W), F32),
            pltpu.VMEM((2, 2, OWN, 2 * W, W), F32),
            pltpu.VMEM((OWN, 2 * W, W), F32),
            pltpu.VMEM(quarter, BF),
            pltpu.VMEM(quarter, BF),
            pltpu.VMEM(quarter, F32),
            pltpu.VMEM((2 * NB, W, W), F32),
            pltpu.VMEM((SIDE * SLAB, 2 * W), F32),
            dma((3,)), dma((3,)), dma((4,)), dma((4,)),
            dma((NEAR, 3)), dma((NEAR, 3)), dma((NEAR, 15)), dma((NEAR, 15)), dma((NEAR, 15)), dma((NEAR, 15)),
            dma((NEAR, 3)), dma((NEAR, 3)), dma((NEAR,)), dma((NEAR,)),
            dma((2,)), dma((2,)), dma((2, OWN)), dma((2, OWN)), dma((3, 3)), dma((3, 3)), dma((4, 3)), dma((4, 3)),
        ],
        compiler_params=pltpu.CompilerParams(
            collective_id=0, has_side_effects=True, vmem_limit_bytes=46 * 2**20
        ),
    )(partners, matrix)


def solution(mesh):
    placed = (P("rows", "cols"), P())
    return jax.shard_map(
        body, mesh=mesh, in_specs=placed, out_specs=P("rows", "cols"), check_vma=False
    )
```
